512 devices in a mesh: section: 16 (over x_hi, z), peer: 32 (over y, x_lo, core).
Axes of the slice: x: 4 (x_hi: 2, x_lo: 2; x = x_hi * 2 + x_lo), y: 8, z: 8, core: 2. Of those that a mesh axis runs over, the one named last changes fastest.
Arguments:
- acts: bfloat16 [16, 32, 2, 64, 2560], P('section', 'peer'), may hold values from -6 to 6
- cotangent: bfloat16 [16, 32, 2, 64, 2560], P('section', 'peer'), may hold values from -6 to 6
- gain: float32 [16, 2560], P('section'), may hold values from 0.1 to 1.9
- w_down: bfloat16 [16, 2560, 128], P('section'), may hold values from -0.125 to 0.125
- w_up: bfloat16 [16, 128, 2560], P('section'), may hold values from -0.5 to 0.5
- route_fwd: int32 [16, 32, 2], P('section', 'peer'), may hold values from 0 to 31, as said below
- route_bwd: int32 [16, 32, 2], P('section', 'peer'), may hold values from 0 to 31, as said below
- token_counts: int32 [16, 32, 2], P('section', 'peer'), may hold values from 1 to 64, as said below
Outputs:
- arrived_act: bfloat16 [16, 32, 3, 64, 2560], P('section', 'peer')
- arrived_grad: bfloat16 [16, 32, 3, 64, 2560], P('section', 'peer')
- grad_down: float32 [16, 2560, 128], P('section', 'peer')
- grad_up: float32 [16, 128, 2560], P('section', None, 'peer')
- grad_gain: float32 [16, 2560], P('section', 'peer')
The draws below stay inside these ranges and needn't reach their ends.
Inputs may be any that keep to these rules, and one draw needn't show every extreme that they name: route_fwd[s, p, j] is a peer of section s + 1; the 2 entries of one peer differ; at every section boundary no peer is named more than 3 times and some peer exactly 3 times. route_bwd[s, p, j] is a peer of section s - 1, with the same rules as route_fwd. `token_counts`: some micro-batch holds exactly 64 live tokens.
All inputs are finite; a program needn't handle non-finite values.
Results may differ from the reference program's by a relative error of at most 0.0053.
Values may be sent and summed in bfloat16 or wider, within the bound.
A program may use at most 128 MiB of HBM per device.

```python
import jax
import jax.numpy as jnp
from jax import lax

D = 2560
R = 128
MB = 2
MBT = 64
SECTIONS = 16
PEERS = 32
CAP = 3


def routing_table(table_key):

    def one_section(section_key):
        key_order, key_relabel = jax.random.split(section_key)
        shuffle = jax.random.permutation(key_order, PEERS)
        relabel = jax.random.permutation(key_relabel, PEERS)
        peer_index = jnp.arange(PEERS, dtype=jnp.int32)
        base_slot = jnp.where(peer_index < MB, peer_index // 2, peer_index - MB // 2)
        first_slot = base_slot[shuffle]
        slot_table = (first_slot[:, None] + jnp.arange(MB, dtype=jnp.int32)[None, :]) % PEERS
        return relabel[slot_table].astype(jnp.int32)
    return jax.vmap(one_section)(jax.random.split(table_key, SECTIONS))


def draw_route_fwd(key, part):
    key = jax.random.fold_in(key, 11)
    return routing_table(key)


def draw_route_bwd(key, part):
    key = jax.random.fold_in(key, 23)
    return routing_table(key)


def draw_token_counts(key, part):
    key = jax.random.fold_in(key, 37)
    count_key, chosen_key = jax.random.split(key)
    counts = jax.random.randint(count_key, (SECTIONS * PEERS * MB,), 1, MBT + 1)
    chosen = jax.random.randint(chosen_key, (), 0, SECTIONS * PEERS * MB)
    flat_counts = jnp.where(jnp.arange(SECTIONS * PEERS * MB) == chosen, MBT, counts)
    return flat_counts.reshape(SECTIONS, PEERS, MB).astype(jnp.int32)


def block_levels(rng, shape, pieces, smallest, largest):
    level, own = 1.0, jax.random.fold_in(rng, 6)
    for dim, shards_of in pieces:
        draws = jnp.exp(jax.random.uniform(jax.random.fold_in(own, dim), (shards_of,), jnp.float32, smallest / len(pieces), largest / len(pieces)))
        level = level * jnp.repeat(draws, shape[dim] // shards_of).reshape([-1 if axis == dim else 1 for axis in range(len(shape))])
    return level


def bell_draw(key, extent, scale, limit, shards=(), kind=jnp.bfloat16):
    values = scale * jax.random.normal(key, extent, jnp.float32)
    if shards:
        values = values * block_levels(key, extent, shards, -0.22, 0.18)
    return jnp.clip(values, -limit, limit).astype(kind)


def setup_inputs(seed: int = 0) -> dict:
    keys = jax.random.split(jax.random.key(seed), 9)
    return {
        "acts": bell_draw(keys[0], (SECTIONS, PEERS, MB, MBT, D), 1.0, 6.0, ((0, 16), (1, 32))),
        "cotangent": bell_draw(keys[1], (SECTIONS, PEERS, MB, MBT, D), 1.0, 6.0, ((0, 16), (1, 32))),
        "gain": jnp.clip(1.0 + 0.18 * jax.random.normal(keys[2], (SECTIONS, D), jnp.float32), 0.1, 1.9),
        "w_down": bell_draw(keys[3], (SECTIONS, D, R), D ** -0.5, 0.125, ((0, 16),)),
        "w_up": bell_draw(keys[4], (SECTIONS, R, D), R ** -0.5, 0.5, ((0, 16),)),
        "route_fwd": draw_route_fwd(jax.random.fold_in(keys[8], 71), 0),
        "route_bwd": draw_route_bwd(jax.random.fold_in(keys[8], 71), 0),
        "token_counts": draw_token_counts(jax.random.fold_in(keys[8], 71), 0),
    }


epsilon = 1e-05

def adapter_forward(rows, token_mask, gain_row, down_proj, up_proj):
    widened = rows.astype(jnp.float32)
    inverse = lax.rsqrt(lax.optimization_barrier(jnp.mean(widened * widened, axis=-1, keepdims=True)) + epsilon)
    unit_rows = widened * inverse
    normed = (unit_rows * gain_row[None, :]).astype(jnp.bfloat16)
    before = jnp.dot(normed, down_proj, preferred_element_type=jnp.float32)
    active = jax.nn.silu(before).astype(jnp.bfloat16)
    branch = jnp.dot(active, up_proj, preferred_element_type=jnp.float32)
    outputs = ((widened + branch) * token_mask[:, None]).astype(jnp.bfloat16)
    return (outputs, (inverse, unit_rows, normed, before, active))

def adapter_backward(incoming, token_mask, gain_row, down_proj, up_proj, saved_state):
    inverse, unit_rows, normed, before, active = saved_state
    masked = incoming * token_mask[:, None].astype(jnp.bfloat16)
    up_total = jnp.dot(active.T, masked, preferred_element_type=jnp.float32)
    act_grad = jnp.dot(masked, up_proj.T, preferred_element_type=jnp.float32)
    sig_value = jax.nn.sigmoid(before)
    pre_grad = (act_grad * sig_value * (1.0 + before * (1.0 - sig_value))).astype(jnp.bfloat16)
    down_total = jnp.dot(normed.T, pre_grad, preferred_element_type=jnp.float32)
    norm_grad = jnp.dot(pre_grad, down_proj.T, preferred_element_type=jnp.float32)
    gain_total = lax.optimization_barrier(jnp.sum(norm_grad * unit_rows, axis=0))
    unit_grad = norm_grad * gain_row[None, :]
    input_grad = masked.astype(jnp.float32) + inverse * (unit_grad - unit_rows * lax.optimization_barrier(jnp.mean(unit_grad * unit_rows, axis=-1, keepdims=True)))
    return (input_grad.astype(jnp.bfloat16), down_total, up_total, gain_total)

def route_section(section_values):
    values, targets = section_values
    receivers = jnp.arange(PEERS, dtype=jnp.int32)
    hit_table = (targets[None, :, :] == receivers[:, None, None]).astype(jnp.float32)
    present = lax.optimization_barrier(jnp.sum(hit_table, axis=2))
    position = jnp.cumsum(present, axis=1) - 1.0
    slot_ids = jnp.arange(CAP, dtype=jnp.float32)
    pick_table = (position[:, None, :] == slot_ids[None, :, None]).astype(jnp.float32) * present[:, None, :]
    weights = pick_table[:, :, :, None] * hit_table[:, None, :, :]
    return jnp.einsum('rkqj,qjtd->rktd', weights, values.astype(jnp.float32)).astype(jnp.bfloat16)

def reference(acts, cotangent, gain, w_down, w_up, route_fwd, route_bwd, token_counts):
    positions = jnp.arange(MBT, dtype=jnp.int32)

    def one_section(section_data):
        section_acts, section_cot, gain_row, down_proj, up_proj, counts = section_data
        token_mask = (positions[None, None, :] < counts[:, :, None]).astype(jnp.float32).reshape(-1)
        flat_rows = section_acts.reshape(-1, D)
        outputs, saved_state = adapter_forward(flat_rows, token_mask, gain_row, down_proj, up_proj)
        input_grad, down_total, up_total, gain_total = adapter_backward(section_cot.reshape(-1, D), token_mask, gain_row, down_proj, up_proj, saved_state)
        grid_shape = section_acts.shape
        return (outputs.reshape(grid_shape), input_grad.reshape(grid_shape), down_total / PEERS, up_total / PEERS, gain_total / PEERS)
    outputs, input_grad, grad_down, grad_up, grad_gain = lax.map(one_section, (acts, cotangent, gain, w_down, w_up, token_counts))
    sent_forward = lax.map(route_section, (outputs, route_fwd))
    sent_backward = lax.map(route_section, (input_grad, route_bwd))
    empty_section = jnp.zeros((1, PEERS, CAP, MBT, D), jnp.bfloat16)
    arrived_act = jnp.concatenate([empty_section, sent_forward[:-1]], axis=0)
    arrived_grad = jnp.concatenate([sent_backward[1:], empty_section], axis=0)
    return (arrived_act, arrived_grad, grad_down, grad_up, grad_gain)
```

```python
import functools

import jax
import jax.numpy as jnp
from jax import lax
from jax.experimental import pallas as pl
from jax.experimental.pallas import tpu as pltpu
from jax.sharding import PartitionSpec as P

epsilon = 1e-05
MESH = pl.DeviceIdType.MESH
f32, bf16, i32 = jnp.float32, jnp.bfloat16, jnp.int32


def matmul(a, b, contract_a, contract_b):
    return lax.dot_general(
        a, b, (((contract_a,), (contract_b,)), ((), ())), preferred_element_type=f32
    )


def arrived(ref, sem):
    pltpu.make_async_copy(ref, ref, sem).wait()


def kernel(
    sections, peers, cap,
    route_fwd, route_bwd, counts, x_ref, cot_ref, gain_ref, down_ref, up_ref,
    act_out, grad_out, gdown_out, gup_out, ggain_out,
    normed, masked, norm_grad, inverse, gain_acc,
    src_f, src_b, mid_f, mid_b, pick_f, pick_b,
    tile_f, tile_b, tiles_f, tiles_b, table_v, table_f, table_b,
    piece, from_core, from_x, chain_a, chain_b,
    p1_send, p1_recv, swap_send, swap_recv, tile_send, tile_recv,
    tswap_send, tswap_recv, table_sem, p2_send, p2_recv,
    core_send, core_recv, x_send, x_recv, a_send, a_recv, b_send, b_recv,
):
    rows, width = x_ref.shape
    units = up_ref.shape[0]
    spread, batches, group, span = src_f.shape
    ring = spread // 2
    column_groups = width // span
    row_groups = spread // column_groups
    share = width // peers
    length = rows // batches

    s, p = lax.axis_index("section"), lax.axis_index("peer")
    c, m = p % 2, p // 2
    x, y = m % 2, m // 2
    sibling = p + 1 - 2 * c
    has_next = s < sections - 1
    has_prev = s > 0

    def partner(i):
        k = i // 2
        odd = k % 2
        step = odd * ((k + 1) // 2) + (1 - odd) * (ring - k // 2)
        return ((y + step) % ring) * 2 + (x + i) % 2

    barrier = pltpu.get_barrier_semaphore()

    def greet(i, carry):
        q = 2 * partner(i) + c

        @pl.when(has_next)
        def _():
            pl.semaphore_signal(barrier, inc=1, device_id=(s + 1, q), device_id_type=MESH)

        @pl.when(has_prev)
        def _():
            pl.semaphore_signal(barrier, inc=1, device_id=(s - 1, q), device_id_type=MESH)

        @pl.when(i > 0)
        def _():
            pl.semaphore_signal(barrier, inc=1, device_id=(s, q), device_id_type=MESH)

        return carry

    lax.fori_loop(0, spread, greet, 0)
    pl.semaphore_signal(barrier, inc=1, device_id=(s, sibling), device_id_type=MESH)

    row_ids = lax.broadcasted_iota(i32, (rows, 1), 0)
    limit = jnp.where(row_ids < length, counts[0], counts[1] + length)
    mask = (row_ids < limit).astype(f32)
    mask_small = mask.astype(bf16)

    def normalise(g, carry):
        here = pl.ds(pl.multiple_of(g * group, group), group)
        widened = x_ref[here, :].astype(f32)
        inv = lax.rsqrt(jnp.sum(widened * widened, axis=-1, keepdims=True) / width + epsilon)
        inverse[here, :] = inv
        normed[here, :] = (widened * inv * gain_ref[...]).astype(bf16)
        return carry

    lax.fori_loop(0, rows // group, normalise, 0, unroll=2)
    before = matmul(normed[...], down_ref[...], 1, 0)
    sig = jax.nn.sigmoid(before)
    active = (before * sig).astype(bf16)
    for k in range(column_groups):
        here = slice(k * span, (k + 1) * span)
        branch = matmul(active, up_ref[:, here], 1, 0)
        outputs = ((x_ref[:, here].astype(f32) + branch) * mask).astype(bf16)
        for g in range(rows // group):
            j, t = g // row_groups, g % row_groups
            src_f[t * column_groups + k, j] = outputs[g * group : (g + 1) * group]

    lane_rows = lax.broadcasted_iota(i32, tile_f.shape, 0)
    tile_f[...] = jnp.where(lane_rows == 0, route_fwd[0], route_fwd[1])
    tile_b[...] = jnp.where(lane_rows == 0, route_bwd[0], route_bwd[1])

    others = has_next.astype(i32) + has_prev.astype(i32) + 1
    pl.semaphore_wait(barrier, spread * others)

    def slots(origin):
        return pl.ds(1 + (c * spread + origin) * batches, batches)

    def spread_out(way, section, src, mid, tile, tiles):
        def tile_step(i, carry):
            pltpu.make_async_remote_copy(
                src_ref=tile, dst_ref=tiles.at[c, m],
                send_sem=tile_send.at[way], recv_sem=tile_recv.at[way],
                device_id=(section, 2 * partner(i) + c), device_id_type=MESH,
            ).start()
            return carry

        def step(i, carry):
            to = partner(i)
            pltpu.make_async_remote_copy(
                src_ref=src.at[to], dst_ref=mid.at[slots(m)],
                send_sem=p1_send.at[way], recv_sem=p1_recv.at[way, m],
                device_id=(section, 2 * to + c), device_id_type=MESH,
            ).start()
            return carry

        lax.fori_loop(0, spread, step, 0)
        lax.fori_loop(0, spread, tile_step, 0)

    @pl.when(has_next)
    def _():
        spread_out(0, s + 1, src_f, mid_f, tile_f, tiles_f)

    masked[...] = cot_ref[...] * mask_small
    act_grad = matmul(masked[...], up_ref[...], 1, 1)
    pre_grad = (act_grad * sig * (1.0 + before * (1.0 - sig))).astype(bf16)
    for k in range(column_groups):
        here = slice(k * span, (k + 1) * span)
        norm_grad[:, here] = matmul(pre_grad, down_ref[here, :], 1, 1)
    gain_acc[...] = jnp.zeros_like(gain_acc)

    def input_grad(g, carry):
        here = pl.ds(pl.multiple_of(g * group, group), group)
        inv = inverse[here, :]
        unit = x_ref[here, :].astype(f32) * inv
        ng = norm_grad[here, :]
        product = ng * unit
        gain_acc[...] += product[: group // 2] + product[group // 2 :]
        scaled = ng * gain_ref[...]
        mean = jnp.sum(scaled * unit, axis=-1, keepdims=True) / width
        grad = (masked[here, :].astype(f32) + inv * (scaled - unit * mean)).astype(bf16)
        for k in range(column_groups):
            src_b[(g % row_groups) * column_groups + k, g // row_groups] = grad[
                :, k * span : (k + 1) * span
            ]
        return carry

    lax.fori_loop(0, rows // group, input_grad, 0)

    @pl.when(has_prev)
    def _():
        spread_out(1, s - 1, src_b, mid_b, tile_b, tiles_b)

    per_group = span // share
    for k in range(column_groups):
        here = slice(k * span, (k + 1) * span)
        down_part = matmul(normed[:, here], pre_grad, 0, 0)
        up_part = matmul(masked[:, here], active, 0, 0)
        for i in range(per_group):
            q = k * per_group + i
            own = (q % 2, (q // 2) % 2, q // 4)
            mine = slice(i * share, (i + 1) * share)
            piece[own + (slice(0, share),)] = down_part[mine]
            piece[own + (slice(share, 2 * share),)] = up_part[mine]
            gains = gain_acc[:, q * share : (q + 1) * share]
            blank = jnp.zeros((gains.shape[0], units - share), f32)
            piece[own + (slice(2 * share, 2 * share + 8),)] = jnp.concatenate([gains, blank], axis=1)

    def to_core(k, half):
        return pltpu.make_async_remote_copy(
            src_ref=piece.at[1 - c, half], dst_ref=from_core.at[half],
            send_sem=core_send.at[k], recv_sem=core_recv.at[k],
            device_id=(s, sibling), device_id_type=MESH,
        )

    to_core(0, 1 - x).start()
    to_core(1, x).start()

    def add_core(k, half):
        arrived(from_core.at[half], core_recv.at[k])

        def step(i, carry):
            piece[c, half, i] += from_core[half, i]
            return carry

        lax.fori_loop(0, ring, step, 0)

    add_core(0, 1 - x)
    to_x = pltpu.make_async_remote_copy(
        src_ref=piece.at[c, 1 - x], dst_ref=from_x,
        send_sem=x_send, recv_sem=x_recv,
        device_id=(s, 2 * (m + 1 - 2 * x) + c), device_id_type=MESH,
    )
    to_x.start()
    add_core(1, x)

    def swap(way, mid, tiles):
        def step(i, carry):
            origin = partner(i)
            here = mid.at[slots(origin)]
            arrived(here, p1_recv.at[way, origin])
            pltpu.make_async_remote_copy(
                src_ref=here, dst_ref=here,
                send_sem=swap_send.at[way], recv_sem=swap_recv.at[way],
                device_id=(s, sibling), device_id_type=MESH,
            ).start()
            return carry

        lax.fori_loop(0, spread, step, 0)
        arrived(tiles.at[c], tile_recv.at[way])
        pltpu.make_async_remote_copy(
            src_ref=tiles.at[c], dst_ref=tiles.at[c],
            send_sem=tswap_send.at[way], recv_sem=tswap_recv.at[way],
            device_id=(s, sibling), device_id_type=MESH,
        ).start()

    def half_of(mid, core):
        return mid.at[pl.ds(1 + core * spread * batches, spread * batches)]

    def deliver(way, mid, tiles, table, pick, out):
        arrived(tiles.at[1 - c], tswap_recv.at[way])
        lanes = lax.broadcasted_iota(i32, (1, tiles.shape[3]), 1)

        def count(i, carry):
            seen, chosen = carry
            for core in range(2):
                for j in range(batches):
                    hit = tiles[core, i, j : j + 1, :] == lanes
                    name = 1 + (core * spread + i) * batches + j
                    chosen = tuple(
                        old + jnp.where(hit & (seen == k), name, 0) for k, old in enumerate(chosen)
                    )
                    seen = seen + hit.astype(i32)
            return seen, chosen

        table_v[...] = jnp.zeros_like(table_v)
        none = jnp.zeros_like(lanes)
        _, chosen = lax.fori_loop(0, spread, count, (none, (none,) * cap))
        for k in range(cap):
            table_v[k : k + 1, :] = chosen[k]
        to_table = pltpu.make_async_copy(table_v, table, table_sem.at[way])
        to_table.start()
        mid[0] = jnp.zeros(mid.shape[1:], bf16)
        to_table.wait()
        arrived(half_of(mid, 1 - c), swap_recv.at[way])

        tokens = pl.ds(pl.multiple_of((m // column_groups) * group, group), group)
        columns = pl.ds(pl.multiple_of((m % column_groups) * span, 128), span)

        def step(i, carry):
            to = partner(i)
            for k in range(cap):
                pick[to, k] = mid[table[k, 2 * to + c]]
            pltpu.make_async_remote_copy(
                src_ref=pick.at[to], dst_ref=out.at[:, tokens, columns],
                send_sem=p2_send.at[way], recv_sem=p2_recv.at[way],
                device_id=(s, 2 * to + c), device_id_type=MESH,
            ).start()
            return carry

        lax.fori_loop(1, spread, step, 0)
        for k in range(cap):
            out[k, tokens, columns] = mid[table[k, p]]

    def settle(way, mid, tiles, pick):
        arrived(pick.at[pl.ds(0, spread - 1)], p2_recv.at[way])
        arrived(pick.at[pl.ds(0, spread - 1)], p2_send.at[way])
        arrived(half_of(mid, c), swap_send.at[way])
        arrived(tiles.at[c], tswap_send.at[way])

    @pl.when(has_prev)
    def _():
        swap(0, mid_f, tiles_f)
        deliver(0, mid_f, tiles_f, table_f, pick_f, act_out)

    @pl.when(s == 0)
    def _():
        act_out[...] = jnp.zeros_like(act_out)

    turn = 1 - 2 * c
    far_a, far_b = ring // 2, ring - 1 - ring // 2

    def along(step):
        return (y + ring + step) % ring

    def chain_step(t, far, way, hold, send, recv):
        at = along(way * (far - t))
        if t > 0:
            arrived(hold.at[t - 1], recv.at[t - 1])
            piece[c, x, at] += hold[t - 1]
        pltpu.make_async_remote_copy(
            src_ref=piece.at[c, x, at], dst_ref=hold.at[t],
            send_sem=send.at[t], recv_sem=recv.at[t],
            device_id=(s, 4 * along(way) + 2 * x + c), device_id_type=MESH,
        ).start()

    arrived(from_x, x_recv)

    def add_x(i, carry):
        piece[c, x, i] += from_x[i]
        return carry

    lax.fori_loop(0, ring, add_x, 0)

    def both(t):
        if t < far_a:
            chain_step(t, far_a, turn, chain_a, a_send, a_recv)
        if t < far_b:
            chain_step(t, far_b, -turn, chain_b, b_send, b_recv)

    both(0)

    @pl.when(has_next)
    def _():
        swap(1, mid_b, tiles_b)

    for t in range(1, far_a):
        both(t)

    @pl.when(has_next)
    def _():
        deliver(1, mid_b, tiles_b, table_b, pick_b, grad_out)

    @pl.when(s == sections - 1)
    def _():
        grad_out[...] = jnp.zeros_like(grad_out)

    arrived(chain_a.at[far_a - 1], a_recv.at[far_a - 1])
    total = piece[c, x, y] + chain_a[far_a - 1]
    if far_b:
        arrived(chain_b.at[far_b - 1], b_recv.at[far_b - 1])
        total = total + chain_b[far_b - 1]
    total = total * (1.0 / peers)
    gdown_out[...] = total[:share]
    gup_out[...] = total[share : 2 * share].T
    ggain_out[...] = jnp.sum(total[2 * share :, :share], axis=0, keepdims=True)

    for k, half in enumerate((1 - x, x)):
        arrived(from_core.at[half], core_send.at[k])
    arrived(from_x, x_send)
    for t in range(far_a):
        arrived(chain_a.at[t], a_send.at[t])
    for t in range(far_b):
        arrived(chain_b.at[t], b_send.at[t])

    @pl.when(has_next)
    def _():
        arrived(src_f, p1_send.at[0])
        arrived(tiles_f.at[0], tile_send.at[0])

    @pl.when(has_prev)
    def _():
        arrived(src_b, p1_send.at[1])
        arrived(tiles_b.at[0], tile_send.at[1])

    @pl.when(has_prev)
    def _():
        settle(0, mid_f, tiles_f, pick_f)

    @pl.when(has_next)
    def _():
        settle(1, mid_b, tiles_b, pick_b)


def on_device(sections, peers, acts, cotangent, gain, w_down, w_up, route_fwd, route_bwd, token_counts):
    batches, length, width = acts.shape[2:]
    units = w_up.shape[1]
    cap = batches + batches // 2
    rows = batches * length
    spread = peers // 2
    ring = spread // 2
    group = 16
    span = width // (spread // (length // group))
    share = width // peers
    height = 2 * share + 8
    far_a, far_b = ring // 2, max(ring - 1 - ring // 2, 1)
    vmem, smem = pltpu.VMEM, pltpu.SMEM
    dma, pair = pltpu.SemaphoreType.DMA, pltpu.SemaphoreType.DMA((2,))
    in_vmem, in_smem = pl.BlockSpec(memory_space=vmem), pl.BlockSpec(memory_space=smem)
    mid = vmem((1 + 2 * spread * batches, group, span), bf16)
    pick = vmem((spread, cap, group, span), bf16)
    src = vmem((spread, batches, group, span), bf16)
    results = pl.pallas_call(
        functools.partial(kernel, sections, peers, cap),
        out_shape=(
            jax.ShapeDtypeStruct((cap, length, width), bf16),
            jax.ShapeDtypeStruct((cap, length, width), bf16),
            jax.ShapeDtypeStruct((share, units), f32),
            jax.ShapeDtypeStruct((units, share), f32),
            jax.ShapeDtypeStruct((1, share), f32),
        ),
        in_specs=[in_smem] * 3 + [in_vmem] * 5,
        out_specs=(in_vmem,) * 5,
        scratch_shapes=[
            vmem((rows, width), bf16),
            vmem((rows, width), bf16),
            vmem((rows, width), f32),
            vmem((rows, 1), f32),
            vmem((8, width), f32),
            src, src, mid, mid, pick, pick,
            vmem((8, 128), i32), vmem((8, 128), i32),
            vmem((2, spread, 8, 128), i32), vmem((2, spread, 8, 128), i32),
            vmem((8, 128), i32), smem((8, 128), i32), smem((8, 128), i32),
            vmem((2, 2, ring, height, units), f32),
            vmem((2, ring, height, units), f32),
            vmem((ring, height, units), f32),
            vmem((far_a, height, units), f32),
            vmem((far_b, height, units), f32),
            pair, dma((2, spread)), pair, pair, pair, pair,
            pair, pair, pair, pair, pair,
            pair, pair, dma, dma, dma((far_a,)), dma((far_a,)), dma((far_b,)), dma((far_b,)),
        ],
        compiler_params=pltpu.CompilerParams(
            collective_id=0, has_side_effects=True, vmem_limit_bytes=48 * 1024 * 1024
        ),
        cost_estimate=pl.CostEstimate(
            flops=12 * rows * width * units, bytes_accessed=8 * rows * width, transcendentals=rows * units
        ),
        name="adapter_relay",
    )(
        route_fwd.reshape(batches), route_bwd.reshape(batches), token_counts.reshape(batches),
        acts.reshape(rows, width), cotangent.reshape(rows, width), gain, w_down[0], w_up[0],
    )
    arrived_act, arrived_grad, grad_down, grad_up, grad_gain = results
    return arrived_act[None, None], arrived_grad[None, None], grad_down[None], grad_up[None], grad_gain


def solution(mesh):
    placed = (
        P("section", "peer", None, None, None),
        P("section", "peer", None, None, None),
        P("section", None),
        P("section", None, None),
        P("section", None, None),
        P("section", "peer", None),
        P("section", "peer", None),
        P("section", "peer", None),
    )
    return jax.shard_map(
        functools.partial(on_device, mesh.shape["section"], mesh.shape["peer"]),
        mesh=mesh,
        in_specs=placed,
        out_specs=(
            P("section", "peer", None, None, None),
            P("section", "peer", None, None, None),
            P("section", "peer", None),
            P("section", None, "peer"),
            P("section", "peer"),
        ),
        check_vma=False,
    )
```

```python
import functools

import jax
import jax.numpy as jnp
from jax import lax
from jax.experimental import pallas as pl
from jax.experimental.pallas import tpu as pltpu
from jax.sharding import PartitionSpec as P

epsilon = 1e-05
MESH = pl.DeviceIdType.MESH
f32, bf16, i32 = jnp.float32, jnp.bfloat16, jnp.int32


def matmul(a, b, contract_a, contract_b):
    return lax.dot_general(
        a, b, (((contract_a,), (contract_b,)), ((), ())), preferred_element_type=f32
    )


def arrived(ref, sem):
    pltpu.make_async_copy(ref, ref, sem).wait()


def kernel(
    sections, peers, cap,
    fwd_hbm, bwd_hbm, counts_hbm, x_hbm, cot_hbm, gain_hbm, down_hbm, up_hbm,
    act_out, grad_out, gdown_out, gup_out, ggain_out,
    route_fwd, route_bwd, counts, x_ref, cot_ref, gain_ref, down_ref, up_ref,
    normed, masked, norm_grad, inverse, gain_acc,
    src_f, src_b, hop_f, hop_b, mid_f, mid_b, pick_f, pick_b,
    tile, tiles_hop, tiles_f, tiles_b, table_v, table_f, table_b,
    piece, from_core, from_x, chain_a, chain_b, final, final_gain,
    hello, store_sem, load_sem, p1_send, p1_recv, z_send, z_recv, swap_send, swap_recv,
    tile_send, tile_recv, tz_send, tz_recv, tswap_send, tswap_recv,
    table_sem, p2_send, p2_recv,
    core_send, core_recv, x_send, x_recv, a_send, a_recv, b_send, b_recv,
):
    rows, width = x_ref.shape
    units = up_ref.shape[0]
    spread, batches, group, span = src_f.shape
    ring = spread // 2
    column_groups = width // span
    row_groups = spread // column_groups
    share = width // peers
    length = rows // batches

    s, p = lax.axis_index("section"), lax.axis_index("peer")
    c, m = p % 2, p // 2
    x, y = m % 2, m // 2
    sibling = p + 1 - 2 * c
    has_next = s < sections - 1
    has_prev = s > 0

    loads = [
        pltpu.make_async_copy(here, there, load_sem.at[k])
        for k, (here, there) in enumerate(
            (
                (x_hbm, x_ref), (gain_hbm, gain_ref), (down_hbm, down_ref), (up_hbm, up_ref),
                (counts_hbm, counts), (fwd_hbm, route_fwd), (bwd_hbm, route_bwd), (cot_hbm, cot_ref),
            )
        )
    ]
    for load in loads:
        load.start()

    def partner(i):
        k = i // 2
        odd = k % 2
        step = odd * ((k + 1) // 2) + (1 - odd) * (ring - k // 2)
        return ((y + step) % ring) * 2 + (x + i) % 2

    barrier = pltpu.get_barrier_semaphore()

    def greet(i, carry):
        pl.semaphore_signal(barrier, inc=1, device_id=(s, 2 * partner(i) + c), device_id_type=MESH)
        return carry

    lax.fori_loop(1, spread, greet, 0)
    pl.semaphore_signal(barrier, inc=1, device_id=(s, sibling), device_id_type=MESH)

    @pl.when(has_prev)
    def _():
        pl.semaphore_signal(barrier, inc=1, device_id=(s - 1, p), device_id_type=MESH)

    for load in loads[:7]:
        load.wait()
    row_ids = lax.broadcasted_iota(i32, (rows, 1), 0)
    limit = jnp.where(row_ids < length, counts[0], counts[1] + length)
    mask = (row_ids < limit).astype(f32)
    mask_small = mask.astype(bf16)

    def normalise(g, carry):
        here = pl.ds(pl.multiple_of(g * group, group), group)
        widened = x_ref[here, :].astype(f32)
        inv = lax.rsqrt(jnp.sum(widened * widened, axis=-1, keepdims=True) / width + epsilon)
        inverse[here, :] = inv
        normed[here, :] = (widened * inv * gain_ref[...]).astype(bf16)
        return carry

    lax.fori_loop(0, rows // group, normalise, 0, unroll=2)
    before = matmul(normed[...], down_ref[...], 1, 0)
    sig = jax.nn.sigmoid(before)
    active = (before * sig).astype(bf16)
    for k in range(column_groups):
        here = slice(k * span, (k + 1) * span)
        branch = matmul(active, up_ref[:, here], 1, 0)
        outputs = ((x_ref[:, here].astype(f32) + branch) * mask).astype(bf16)
        for g in range(rows // group):
            j, t = g // row_groups, g % row_groups
            src_f[t * column_groups + k, j] = outputs[g * group : (g + 1) * group]

    kinds = lax.broadcasted_iota(i32, tile.shape, 0)
    routes = jnp.where(
        kinds < 2,
        jnp.where(kinds == 0, route_fwd[0], route_fwd[1]),
        jnp.where(kinds == 2, route_bwd[0], route_bwd[1]),
    )
    tile[...] = routes
    tiles_hop[m] = routes

    pl.semaphore_wait(barrier, spread + has_next.astype(i32))

    @pl.when(has_next)
    def _():
        pl.semaphore_signal(hello, inc=1, device_id=(s + 1, p), device_id_type=MESH)

    def send_tile(i, carry):
        pltpu.make_async_remote_copy(
            src_ref=tile, dst_ref=tiles_hop.at[m], send_sem=tile_send, recv_sem=tile_recv,
            device_id=(s, 2 * partner(i) + c), device_id_type=MESH,
        ).start()
        return carry

    lax.fori_loop(1, spread, send_tile, 0)

    def slots(origin):
        return pl.ds(1 + (c * spread + origin) * batches, batches)

    def shift(way, chunk, origin, mid):
        pltpu.make_async_remote_copy(
            src_ref=chunk, dst_ref=mid.at[slots(origin)],
            send_sem=z_send.at[way], recv_sem=z_recv.at[way, origin],
            device_id=(s + 1 - 2 * way, p), device_id_type=MESH,
        ).start()

    def spread_out(way, src, hop):
        def step(i, carry):
            to = partner(i)
            pltpu.make_async_remote_copy(
                src_ref=src.at[to], dst_ref=hop.at[m],
                send_sem=p1_send.at[way], recv_sem=p1_recv.at[way, m],
                device_id=(s, 2 * to + c), device_id_type=MESH,
            ).start()
            return carry

        lax.fori_loop(1, spread, step, 0)

    @pl.when(has_next)
    def _():
        spread_out(0, src_f, hop_f)
        shift(0, src_f.at[m], m, mid_f)

    loads[7].wait()
    masked[...] = cot_ref[...] * mask_small
    act_grad = matmul(masked[...], up_ref[...], 1, 1)
    pre_grad = (act_grad * sig * (1.0 + before * (1.0 - sig))).astype(bf16)
    for k in range(column_groups):
        here = slice(k * span, (k + 1) * span)
        norm_grad[:, here] = matmul(pre_grad, down_ref[here, :], 1, 1)
    gain_acc[...] = jnp.zeros_like(gain_acc)

    def input_grad(g, carry):
        here = pl.ds(pl.multiple_of(g * group, group), group)
        inv = inverse[here, :]
        unit = x_ref[here, :].astype(f32) * inv
        ng = norm_grad[here, :]
        product = ng * unit
        gain_acc[...] += product[: group // 2] + product[group // 2 :]
        scaled = ng * gain_ref[...]
        mean = jnp.sum(scaled * unit, axis=-1, keepdims=True) / width
        grad = (masked[here, :].astype(f32) + inv * (scaled - unit * mean)).astype(bf16)
        for k in range(column_groups):
            src_b[(g % row_groups) * column_groups + k, g // row_groups] = grad[
                :, k * span : (k + 1) * span
            ]
        return carry

    lax.fori_loop(0, rows // group, input_grad, 0)

    per_group = span // share
    for k in range(column_groups):
        here = slice(k * span, (k + 1) * span)
        down_part = matmul(normed[:, here], pre_grad, 0, 0)
        up_part = matmul(masked[:, here], active, 0, 0)
        for i in range(per_group):
            q = k * per_group + i
            own = (q % 2, (q // 2) % 2, q // 4)
            mine = slice(i * share, (i + 1) * share)
            piece[own + (slice(0, share),)] = down_part[mine]
            piece[own + (slice(share, 2 * share),)] = up_part[mine]
            gains = gain_acc[:, q * share : (q + 1) * share]
            blank = jnp.zeros((gains.shape[0], units - share), f32)
            piece[own + (slice(2 * share, 2 * share + 8),)] = jnp.concatenate([gains, blank], axis=1)

    def to_core(k, half):
        return pltpu.make_async_remote_copy(
            src_ref=piece.at[1 - c, half], dst_ref=from_core.at[half],
            send_sem=core_send.at[k], recv_sem=core_recv.at[k],
            device_id=(s, sibling), device_id_type=MESH,
        )

    to_core(0, 1 - x).start()
    to_core(1, x).start()

    @pl.when(has_prev)
    def _():
        spread_out(1, src_b, hop_b)

    def add_core(k, half):
        arrived(from_core.at[half], core_recv.at[k])

        def step(i, carry):
            piece[c, half, i] += from_core[half, i]
            return carry

        lax.fori_loop(0, ring, step, 0)

    add_core(0, 1 - x)
    to_x = pltpu.make_async_remote_copy(
        src_ref=piece.at[c, 1 - x], dst_ref=from_x,
        send_sem=x_send, recv_sem=x_recv,
        device_id=(s, 2 * (m + 1 - 2 * x) + c), device_id_type=MESH,
    )
    to_x.start()
    add_core(1, x)

    arrived(tiles_hop.at[pl.ds(0, spread - 1)], tile_recv)

    def shift_tiles(way, tiles):
        pltpu.make_async_remote_copy(
            src_ref=tiles_hop, dst_ref=tiles.at[c],
            send_sem=tz_send.at[way], recv_sem=tz_recv.at[way],
            device_id=(s + 1 - 2 * way, p), device_id_type=MESH,
        ).start()

    @pl.when(has_next)
    def _():
        shift_tiles(0, tiles_f)

    @pl.when(has_prev)
    def _():
        pl.semaphore_wait(hello, 1)
        shift_tiles(1, tiles_b)
        shift(1, src_b.at[m], m, mid_b)

    def relay(way, hop, mid, first, last):
        def step(i, carry):
            origin = partner(i)
            arrived(hop.at[origin], p1_recv.at[way, origin])
            shift(way, hop.at[origin], origin, mid)
            return carry

        lax.fori_loop(first, last, step, 0)

    def swap(way, mid, tiles):
        def step(i, carry):
            origin = partner(i)
            here = mid.at[slots(origin)]
            arrived(here, z_recv.at[way, origin])
            pltpu.make_async_remote_copy(
                src_ref=here, dst_ref=here,
                send_sem=swap_send.at[way], recv_sem=swap_recv.at[way],
                device_id=(s, sibling), device_id_type=MESH,
            ).start()
            return carry

        lax.fori_loop(0, spread, step, 0)
        arrived(tiles.at[c], tz_recv.at[way])
        pltpu.make_async_remote_copy(
            src_ref=tiles.at[c], dst_ref=tiles.at[c],
            send_sem=tswap_send.at[way], recv_sem=tswap_recv.at[way],
            device_id=(s, sibling), device_id_type=MESH,
        ).start()

    def chunk_of(out, k):
        tokens = pl.ds(pl.multiple_of((k // column_groups) * group, group), group)
        columns = pl.ds(pl.multiple_of((k % column_groups) * span, 128), span)
        return out.at[:, tokens, columns]

    def keep(way, pick, out, k):
        return pltpu.make_async_copy(pick.at[k], chunk_of(out, k), store_sem.at[way, k])

    def half_of(mid, core):
        return mid.at[pl.ds(1 + core * spread * batches, spread * batches)]

    def deliver(way, mid, tiles, table, pick, out):
        arrived(tiles.at[1 - c], tswap_recv.at[way])
        lanes = lax.broadcasted_iota(i32, (1, tiles.shape[3]), 1)

        def count(i, carry):
            seen, chosen = carry
            for core in range(2):
                for j in range(batches):
                    at = way * batches + j
                    hit = tiles[core, i, at : at + 1, :] == lanes
                    name = 1 + (core * spread + i) * batches + j
                    chosen = tuple(
                        old + jnp.where(hit & (seen == k), name, 0) for k, old in enumerate(chosen)
                    )
                    seen = seen + hit.astype(i32)
            return seen, chosen

        table_v[...] = jnp.zeros_like(table_v)
        none = jnp.zeros_like(lanes)
        _, chosen = lax.fori_loop(0, spread, count, (none, (none,) * cap))
        for k in range(cap):
            table_v[k : k + 1, :] = chosen[k]
        to_table = pltpu.make_async_copy(table_v, table, table_sem.at[way])
        to_table.start()
        mid[0] = jnp.zeros(mid.shape[1:], bf16)
        to_table.wait()
        arrived(half_of(mid, 1 - c), swap_recv.at[way])

        def step(i, carry):
            to = partner(i)
            for k in range(cap):
                pick[to, k] = mid[table[k, 2 * to + c]]
            pltpu.make_async_remote_copy(
                src_ref=pick.at[to], dst_ref=chunk_of(out, m),
                send_sem=p2_send.at[way], recv_sem=p2_recv.at[way],
                device_id=(s, 2 * to + c), device_id_type=MESH,
            ).start()
            return carry

        lax.fori_loop(1, spread, step, 0)
        for k in range(cap):
            pick[m, k] = mid[table[k, p]]
        keep(way, pick, out, m).start()

    def clear(way, pick, out):
        def fill(k, carry):
            pick[k] = jnp.zeros(pick.shape[1:], bf16)
            keep(way, pick, out, k).start()
            return carry

        def finish(k, carry):
            keep(way, pick, out, k).wait()
            return carry

        lax.fori_loop(0, spread, fill, 0)
        lax.fori_loop(0, spread, finish, 0)

    turn = 1 - 2 * c
    far_a, far_b = ring // 2, ring - 1 - ring // 2

    def along(step):
        return (y + ring + step) % ring

    def chain_step(t, far, way, hold, send, recv):
        at = along(way * (far - t))
        if t > 0:
            arrived(hold.at[t - 1], recv.at[t - 1])
            piece[c, x, at] += hold[t - 1]
        pltpu.make_async_remote_copy(
            src_ref=piece.at[c, x, at], dst_ref=hold.at[t],
            send_sem=send.at[t], recv_sem=recv.at[t],
            device_id=(s, 4 * along(way) + 2 * x + c), device_id_type=MESH,
        ).start()

    def chains(t):
        if t < far_a:
            chain_step(t, far_a, turn, chain_a, a_send, a_recv)
        if t < far_b:
            chain_step(t, far_b, -turn, chain_b, b_send, b_recv)

    def add_x():
        arrived(from_x, x_recv)

        def step(i, carry):
            piece[c, x, i] += from_x[i]
            return carry

        lax.fori_loop(0, ring, step, 0)

    @pl.when(has_next)
    def _():
        relay(0, hop_f, mid_f, 1, spread)

    @pl.when(has_prev)
    def _():
        relay(1, hop_b, mid_b, 1, spread)

    add_x()
    chains(0)

    @pl.when(has_prev)
    def _():
        swap(0, mid_f, tiles_f)

    chains(1)

    @pl.when(has_prev)
    def _():
        deliver(0, mid_f, tiles_f, table_f, pick_f, act_out)

    @pl.when(s == 0)
    def _():
        clear(0, pick_f, act_out)

    chains(2)

    @pl.when(has_next)
    def _():
        swap(1, mid_b, tiles_b)

    chains(3)

    @pl.when(has_next)
    def _():
        deliver(1, mid_b, tiles_b, table_b, pick_b, grad_out)

    @pl.when(s == sections - 1)
    def _():
        clear(1, pick_b, grad_out)


    arrived(chain_a.at[far_a - 1], a_recv.at[far_a - 1])
    total = piece[c, x, y] + chain_a[far_a - 1]
    if far_b:
        arrived(chain_b.at[far_b - 1], b_recv.at[far_b - 1])
        total = total + chain_b[far_b - 1]
    total = total * (1.0 / peers)
    final[...] = total
    final_gain[...] = jnp.sum(total[2 * share :, :share], axis=0, keepdims=True)
    stores = (
        pltpu.make_async_copy(final.at[pl.ds(0, share)], gdown_out, load_sem.at[0]),
        pltpu.make_async_copy(final.at[pl.ds(share, share)], gup_out, load_sem.at[1]),
        pltpu.make_async_copy(final_gain, ggain_out, load_sem.at[2]),
    )
    for store in stores:
        store.start()

    for k, half in enumerate((1 - x, x)):
        arrived(from_core.at[half], core_send.at[k])
    arrived(from_x, x_send)
    for t in range(far_a):
        arrived(chain_a.at[t], a_send.at[t])
    for t in range(far_b):
        arrived(chain_b.at[t], b_send.at[t])
    arrived(tiles_hop.at[pl.ds(0, spread - 1)], tile_send)

    for store in stores:
        store.wait()

    def settle_out(way, src):
        arrived(src.at[pl.ds(0, spread - 1)], p1_send.at[way])
        arrived(src, z_send.at[way])
        arrived(tiles_hop, tz_send.at[way])

    def settle_in(way, mid, tiles, pick, out):
        keep(way, pick, out, m).wait()
        arrived(half_of(mid, c), swap_send.at[way])
        arrived(tiles.at[c], tswap_send.at[way])
        arrived(pick.at[pl.ds(0, spread - 1)], p2_send.at[way])
        arrived(pick.at[pl.ds(0, spread - 1)], p2_recv.at[way])

    @pl.when(has_next)
    def _():
        settle_out(0, src_f)

    @pl.when(has_prev)
    def _():
        settle_out(1, src_b)

    @pl.when(has_prev)
    def _():
        settle_in(0, mid_f, tiles_f, pick_f, act_out)

    @pl.when(has_next)
    def _():
        settle_in(1, mid_b, tiles_b, pick_b, grad_out)


def place(*refs):
    count = (len(refs) - 2) // 3
    given, results, held = (refs[k * count : (k + 1) * count] for k in range(3))
    load_sem, store_sem = refs[-2:]
    loads = [pltpu.make_async_copy(given[k], held[k], load_sem.at[k]) for k in range(count)]
    stores = [pltpu.make_async_copy(held[k], results[k], store_sem.at[k]) for k in range(count)]
    for load in loads:
        load.start()
    for load, store in zip(loads, stores):
        load.wait()
        store.start()
    for store in stores:
        store.wait()


def on_device(sections, peers, acts, cotangent, gain, w_down, w_up, route_fwd, route_bwd, token_counts):
    batches, length, width = acts.shape[2:]
    units = w_up.shape[1]
    cap = batches + batches // 2
    rows = batches * length
    spread = peers // 2
    ring = spread // 2
    group = 16
    span = width // (spread // (length // group))
    share = width // peers
    height = 2 * share + 8
    far_a, far_b = ring // 2, max(ring - 1 - ring // 2, 1)
    vmem, smem = pltpu.VMEM, pltpu.SMEM
    dma, pair = pltpu.SemaphoreType.DMA, pltpu.SemaphoreType.DMA((2,))
    in_hbm = pl.BlockSpec(memory_space=pltpu.HBM)
    mid = vmem((1 + 2 * spread * batches, group, span), bf16)
    pick = vmem((spread, cap, group, span), bf16)
    src = vmem((spread, batches, group, span), bf16)
    shapes = (
        jax.ShapeDtypeStruct((cap, length, width), bf16),
        jax.ShapeDtypeStruct((cap, length, width), bf16),
        jax.ShapeDtypeStruct((share, units), f32),
        jax.ShapeDtypeStruct((share, units), f32),
        jax.ShapeDtypeStruct((1, share), f32),
    )
    results = pl.pallas_call(
        functools.partial(kernel, sections, peers, cap),
        out_shape=shapes,
        in_specs=[in_hbm] * 8,
        out_specs=(in_hbm,) * 5,
        scratch_shapes=[
            smem((batches,), i32), smem((batches,), i32), smem((batches,), i32),
            vmem((rows, width), bf16), vmem((rows, width), bf16), vmem((1, width), f32),
            vmem((width, units), bf16), vmem((units, width), bf16),
            vmem((rows, width), bf16),
            vmem((rows, width), bf16),
            vmem((rows, width), f32),
            vmem((rows, 1), f32),
            vmem((8, width), f32),
            src, src, src, src, mid, mid, pick, pick,
            vmem((8, 128), i32), vmem((spread, 8, 128), i32),
            vmem((2, spread, 8, 128), i32), vmem((2, spread, 8, 128), i32),
            vmem((8, 128), i32), smem((8, 128), i32), smem((8, 128), i32),
            vmem((2, 2, ring, height, units), f32),
            vmem((2, ring, height, units), f32),
            vmem((ring, height, units), f32),
            vmem((far_a, height, units), f32),
            vmem((far_b, height, units), f32),
            vmem((height, units), f32), vmem((1, share), f32),
            pltpu.SemaphoreType.REGULAR, dma((2, spread)), dma((8,)), pair, dma((2, spread)), pair, dma((2, spread)), pair, pair,
            dma, dma, pair, pair, pair, pair,
            pair, pair, pair,
            pair, pair, dma, dma, dma((far_a,)), dma((far_a,)), dma((far_b,)), dma((far_b,)),
        ],
        compiler_params=pltpu.CompilerParams(
            collective_id=0, has_side_effects=True, vmem_limit_bytes=60 * 1024 * 1024
        ),
        cost_estimate=pl.CostEstimate(
            flops=12 * rows * width * units, bytes_accessed=8 * rows * width, transcendentals=rows * units
        ),
        name="adapter_relay",
    )(
        route_fwd.reshape(batches), route_bwd.reshape(batches), token_counts.reshape(batches),
        acts.reshape(rows, width), cotangent.reshape(rows, width), gain, w_down[0], w_up[0],
    )
    arrived_act, arrived_grad, grad_down, grad_up, grad_gain = pl.pallas_call(
        place,
        out_shape=shapes,
        in_specs=[in_hbm] * 5,
        out_specs=(in_hbm,) * 5,
        scratch_shapes=[vmem(made.shape, made.dtype) for made in shapes] + [dma((5,)), dma((5,))],
        compiler_params=pltpu.CompilerParams(vmem_limit_bytes=60 * 1024 * 1024),
        name="place_results",
    )(*results)
    return arrived_act[None, None], arrived_grad[None, None], grad_down[None], grad_up.T[None], grad_gain


def solution(mesh):
    placed = (
        P("section", "peer", None, None, None),
        P("section", "peer", None, None, None),
        P("section", None),
        P("section", None, None),
        P("section", None, None),
        P("section", "peer", None),
        P("section", "peer", None),
        P("section", "peer", None),
    )
    return jax.shard_map(
        functools.partial(on_device, mesh.shape["section"], mesh.shape["peer"]),
        mesh=mesh,
        in_specs=placed,
        out_specs=(
            P("section", "peer", None, None, None),
            P("section", "peer", None, None, None),
            P("section", "peer", None),
            P("section", None, "peer"),
            P("section", "peer"),
        ),
        check_vma=False,
    )
```

```python
import functools

import jax
import jax.numpy as jnp
from jax import lax
from jax.experimental import pallas as pl
from jax.experimental.pallas import tpu as pltpu
from jax.sharding import PartitionSpec as P

epsilon = 1e-05
MESH = pl.DeviceIdType.MESH
f32, bf16, i32 = jnp.float32, jnp.bfloat16, jnp.int32


def matmul(a, b, contract_a, contract_b):
    return lax.dot_general(
        a, b, (((contract_a,), (contract_b,)), ((), ())), preferred_element_type=f32
    )


def arrived(ref, sem):
    pltpu.make_async_copy(ref, ref, sem).wait()


def kernel(
    sections, peers, cap,
    fwd_hbm, bwd_hbm, counts_hbm, x_hbm, cot_hbm, gain_hbm, down_hbm, up_hbm,
    act_out, grad_out, gdown_out, gup_out, ggain_out,
    route_fwd, route_bwd, counts, x_ref, cot_ref, gain_ref, down_ref, up_ref,
    normed, masked, norm_grad, inverse, gain_acc,
    src_f, src_b, hop_f, hop_b, mid_f, mid_b, pick_f, pick_b,
    tile, tiles_hop, tiles_f, tiles_b, table_v, table_f, table_b,
    piece, from_core, sum_x, from_x, part_a, part_b, chain_a, chain_b, final, final_gain,
    hello, store_sem, load_sem, p1_send, p1_recv, z_send, z_recv, swap_send, swap_recv,
    tile_send, tile_recv, tz_send, tz_recv, tswap_send, tswap_recv,
    table_sem, p2_send, p2_recv,
    core_send, core_recv, x_send, x_recv, a_send, a_recv, b_send, b_recv,
):
    rows, width = x_ref.shape
    units = up_ref.shape[0]
    spread, batches, group, span = src_f.shape
    ring = spread // 2
    column_groups = width // span
    row_groups = spread // column_groups
    share = width // peers
    length = rows // batches

    s, p = lax.axis_index("section"), lax.axis_index("peer")
    c, m = p % 2, p // 2
    x, y = m % 2, m // 2
    sibling = p + 1 - 2 * c
    has_next = s < sections - 1
    has_prev = s > 0

    loads = [
        pltpu.make_async_copy(here, there, load_sem.at[k])
        for k, (here, there) in enumerate(
            (
                (x_hbm, x_ref), (gain_hbm, gain_ref), (down_hbm, down_ref), (up_hbm, up_ref),
                (counts_hbm, counts), (fwd_hbm, route_fwd), (bwd_hbm, route_bwd), (cot_hbm, cot_ref),
            )
        )
    ]
    for load in loads:
        load.start()

    def partner(i):
        k = i // 2
        odd = k % 2
        step = odd * ((k + 1) // 2) + (1 - odd) * (ring - k // 2)
        return ((y + step) % ring) * 2 + (x + i) % 2

    barrier = pltpu.get_barrier_semaphore()

    def greet(i, carry):
        pl.semaphore_signal(barrier, inc=1, device_id=(s, 2 * partner(i) + c), device_id_type=MESH)
        return carry

    lax.fori_loop(1, spread, greet, 0)
    pl.semaphore_signal(barrier, inc=1, device_id=(s, sibling), device_id_type=MESH)

    @pl.when(has_prev)
    def _():
        pl.semaphore_signal(barrier, inc=1, device_id=(s - 1, p), device_id_type=MESH)

    for load in loads[:7]:
        load.wait()
    row_ids = lax.broadcasted_iota(i32, (rows, 1), 0)
    limit = jnp.where(row_ids < length, counts[0], counts[1] + length)
    mask = (row_ids < limit).astype(f32)
    mask_small = mask.astype(bf16)

    def normalise(g, carry):
        here = pl.ds(pl.multiple_of(g * group, group), group)
        widened = x_ref[here, :].astype(f32)
        inv = lax.rsqrt(jnp.sum(widened * widened, axis=-1, keepdims=True) / width + epsilon)
        inverse[here, :] = inv
        normed[here, :] = (widened * inv * gain_ref[...]).astype(bf16)
        return carry

    lax.fori_loop(0, rows // group, normalise, 0, unroll=2)
    before = matmul(normed[...], down_ref[...], 1, 0)
    sig = jax.nn.sigmoid(before)
    active = (before * sig).astype(bf16)
    for k in range(column_groups):
        here = slice(k * span, (k + 1) * span)
        branch = matmul(active, up_ref[:, here], 1, 0)
        outputs = ((x_ref[:, here].astype(f32) + branch) * mask).astype(bf16)
        for g in range(rows // group):
            j, t = g // row_groups, g % row_groups
            src_f[t * column_groups + k, j] = outputs[g * group : (g + 1) * group]

    kinds = lax.broadcasted_iota(i32, tile.shape, 0)
    routes = jnp.where(
        kinds < 2,
        jnp.where(kinds == 0, route_fwd[0], route_fwd[1]),
        jnp.where(kinds == 2, route_bwd[0], route_bwd[1]),
    )
    tile[...] = routes
    tiles_hop[m] = routes

    pl.semaphore_wait(barrier, spread + has_next.astype(i32))

    @pl.when(has_next)
    def _():
        pl.semaphore_signal(hello, inc=1, device_id=(s + 1, p), device_id_type=MESH)

    def send_tile(i, carry):
        pltpu.make_async_remote_copy(
            src_ref=tile, dst_ref=tiles_hop.at[m], send_sem=tile_send, recv_sem=tile_recv,
            device_id=(s, 2 * partner(i) + c), device_id_type=MESH,
        ).start()
        return carry

    lax.fori_loop(1, spread, send_tile, 0)

    def slots(origin):
        return pl.ds(1 + (c * spread + origin) * batches, batches)

    def shift(way, chunk, origin, mid):
        pltpu.make_async_remote_copy(
            src_ref=chunk, dst_ref=mid.at[slots(origin)],
            send_sem=z_send.at[way], recv_sem=z_recv.at[way, origin],
            device_id=(s + 1 - 2 * way, p), device_id_type=MESH,
        ).start()

    def spread_out(way, src, hop):
        def step(i, carry):
            to = partner(i)
            pltpu.make_async_remote_copy(
                src_ref=src.at[to], dst_ref=hop.at[m],
                send_sem=p1_send.at[way], recv_sem=p1_recv.at[way, m],
                device_id=(s, 2 * to + c), device_id_type=MESH,
            ).start()
            return carry

        lax.fori_loop(1, spread, step, 0)

    def relay(way, hop, mid, first, last):
        def step(i, carry):
            origin = partner(i)
            arrived(hop.at[origin], p1_recv.at[way, origin])
            shift(way, hop.at[origin], origin, mid)
            return carry

        lax.fori_loop(first, last, step, 0)

    @pl.when(has_next)
    def _():
        spread_out(0, src_f, hop_f)
        shift(0, src_f.at[m], m, mid_f)

    loads[7].wait()
    masked[...] = cot_ref[...] * mask_small
    act_grad = matmul(masked[...], up_ref[...], 1, 1)
    pre_grad = (act_grad * sig * (1.0 + before * (1.0 - sig))).astype(bf16)
    for k in range(column_groups):
        here = slice(k * span, (k + 1) * span)
        norm_grad[:, here] = matmul(pre_grad, down_ref[here, :], 1, 1)
    gain_acc[...] = jnp.zeros_like(gain_acc)

    def input_grad(g, carry):
        here = pl.ds(pl.multiple_of(g * group, group), group)
        inv = inverse[here, :]
        unit = x_ref[here, :].astype(f32) * inv
        ng = norm_grad[here, :]
        product = ng * unit
        gain_acc[...] += product
        scaled = ng * gain_ref[...]
        mean = jnp.sum(scaled * unit, axis=-1, keepdims=True) / width
        grad = (masked[here, :].astype(f32) + inv * (scaled - unit * mean)).astype(bf16)
        for k in range(column_groups):
            src_b[(g % row_groups) * column_groups + k, g // row_groups] = grad[
                :, k * span : (k + 1) * span
            ]
        return carry

    lax.fori_loop(0, rows // group, input_grad, 0)

    per_group = span // share
    for k in range(column_groups):
        here = slice(k * span, (k + 1) * span)
        down_part = matmul(normed[:, here], pre_grad, 0, 0)
        up_part = matmul(masked[:, here], active, 0, 0)
        for i in range(per_group):
            q = k * per_group + i
            own = (q % 2, (q // 2) % 2, q // 4)
            mine = slice(i * share, (i + 1) * share)
            piece[own + (slice(0, share),)] = down_part[mine]
            piece[own + (slice(share, 2 * share),)] = up_part[mine]
            gains = gain_acc[:, q * share : (q + 1) * share]
            blank = jnp.zeros((gains.shape[0], units - share), f32)
            piece[own + (slice(2 * share, 2 * share + group),)] = jnp.concatenate([gains, blank], axis=1)

    def to_core(k, half):
        return pltpu.make_async_remote_copy(
            src_ref=piece.at[1 - c, half], dst_ref=from_core.at[half],
            send_sem=core_send.at[k], recv_sem=core_recv.at[k],
            device_id=(s, sibling), device_id_type=MESH,
        )

    to_core(0, 1 - x).start()
    to_core(1, x).start()

    @pl.when(has_prev)
    def _():
        spread_out(1, src_b, hop_b)

    @pl.when(has_next)
    def _():
        relay(0, hop_f, mid_f, 1, 8)

    def add_core(k, half):
        arrived(from_core.at[half], core_recv.at[k])

        def step(i, carry):
            total = piece[c, half, i] + from_core[half, i]
            if k == 0:
                sum_x[i] = total.astype(bf16)
            else:
                piece[c, half, i] = total
            return carry

        lax.fori_loop(0, ring, step, 0)

    add_core(0, 1 - x)
    to_x = pltpu.make_async_remote_copy(
        src_ref=sum_x, dst_ref=from_x,
        send_sem=x_send, recv_sem=x_recv,
        device_id=(s, 2 * (m + 1 - 2 * x) + c), device_id_type=MESH,
    )
    to_x.start()
    add_core(1, x)

    arrived(tiles_hop.at[pl.ds(0, spread - 1)], tile_recv)

    def shift_tiles(way, tiles):
        pltpu.make_async_remote_copy(
            src_ref=tiles_hop, dst_ref=tiles.at[c],
            send_sem=tz_send.at[way], recv_sem=tz_recv.at[way],
            device_id=(s + 1 - 2 * way, p), device_id_type=MESH,
        ).start()

    @pl.when(has_next)
    def _():
        shift_tiles(0, tiles_f)

    @pl.when(has_prev)
    def _():
        pl.semaphore_wait(hello, 1)
        shift_tiles(1, tiles_b)
        shift(1, src_b.at[m], m, mid_b)

    def swap(way, mid, tiles):
        def step(i, carry):
            origin = partner(i)
            here = mid.at[slots(origin)]
            arrived(here, z_recv.at[way, origin])
            pltpu.make_async_remote_copy(
                src_ref=here, dst_ref=here,
                send_sem=swap_send.at[way], recv_sem=swap_recv.at[way],
                device_id=(s, sibling), device_id_type=MESH,
            ).start()
            return carry

        lax.fori_loop(0, spread, step, 0)
        arrived(tiles.at[c], tz_recv.at[way])
        pltpu.make_async_remote_copy(
            src_ref=tiles.at[c], dst_ref=tiles.at[c],
            send_sem=tswap_send.at[way], recv_sem=tswap_recv.at[way],
            device_id=(s, sibling), device_id_type=MESH,
        ).start()

    def chunk_of(out, k):
        tokens = pl.ds(pl.multiple_of((k // column_groups) * group, group), group)
        columns = pl.ds(pl.multiple_of((k % column_groups) * span, 128), span)
        return out.at[:, tokens, columns]

    def keep(way, pick, out, k):
        return pltpu.make_async_copy(pick.at[k], chunk_of(out, k), store_sem.at[way, k])

    def half_of(mid, core):
        return mid.at[pl.ds(1 + core * spread * batches, spread * batches)]

    def look_up(way, mid, tiles, table):
        arrived(tiles.at[1 - c], tswap_recv.at[way])
        lanes = lax.broadcasted_iota(i32, (1, tiles.shape[3]), 1)

        def count(i, carry):
            seen, chosen = carry
            for core in range(2):
                for j in range(batches):
                    at = way * batches + j
                    hit = tiles[core, i, at : at + 1, :] == lanes
                    name = 1 + (core * spread + i) * batches + j
                    chosen = tuple(
                        old + jnp.where(hit & (seen == k), name, 0) for k, old in enumerate(chosen)
                    )
                    seen = seen + hit.astype(i32)
            return seen, chosen

        table_v[...] = jnp.zeros_like(table_v)
        none = jnp.zeros_like(lanes)
        _, chosen = lax.fori_loop(0, spread, count, (none, (none,) * cap))
        for k in range(cap):
            table_v[k : k + 1, :] = chosen[k]
        to_table = pltpu.make_async_copy(table_v, table, table_sem.at[way])
        to_table.start()
        mid[0] = jnp.zeros(mid.shape[1:], bf16)
        to_table.wait()
        arrived(half_of(mid, 1 - c), swap_recv.at[way])

    def deliver(way, mid, table, pick, out, first, last):
        def step(i, carry):
            to = partner(i)
            for k in range(cap):
                pick[to, k] = mid[table[k, 2 * to + c]]
            pltpu.make_async_remote_copy(
                src_ref=pick.at[to], dst_ref=chunk_of(out, m),
                send_sem=p2_send.at[way], recv_sem=p2_recv.at[way],
                device_id=(s, 2 * to + c), device_id_type=MESH,
            ).start()
            return carry

        lax.fori_loop(first, last, step, 0)

    def deliver_own(way, mid, table, pick, out):
        for k in range(cap):
            pick[m, k] = mid[table[k, p]]
        keep(way, pick, out, m).start()

    def clear(way, pick, out):
        def fill(k, carry):
            pick[k] = jnp.zeros(pick.shape[1:], bf16)
            keep(way, pick, out, k).start()
            return carry

        def finish(k, carry):
            keep(way, pick, out, k).wait()
            return carry

        lax.fori_loop(0, spread, fill, 0)
        lax.fori_loop(0, spread, finish, 0)

    turn = 1 - 2 * c
    far_a, far_b = ring // 2, ring - 1 - ring // 2

    def along(step):
        return (y + ring + step) % ring

    def chain_step(t, far, way, part, hold, send, recv):
        total = piece[c, x, along(way * (far - t))]
        if t > 0:
            arrived(hold.at[t - 1], recv.at[t - 1])
            total = total + hold[t - 1].astype(f32)
        part[t] = total.astype(bf16)
        pltpu.make_async_remote_copy(
            src_ref=part.at[t], dst_ref=hold.at[t],
            send_sem=send.at[t], recv_sem=recv.at[t],
            device_id=(s, 4 * along(way) + 2 * x + c), device_id_type=MESH,
        ).start()

    def chains(t):
        if t < far_a:
            chain_step(t, far_a, turn, part_a, chain_a, a_send, a_recv)
        if t < far_b:
            chain_step(t, far_b, -turn, part_b, chain_b, b_send, b_recv)

    def add_x():
        arrived(from_x, x_recv)

        def step(i, carry):
            piece[c, x, i] += from_x[i].astype(f32)
            return carry

        lax.fori_loop(0, ring, step, 0)

    @pl.when(has_next)
    def _():
        relay(0, hop_f, mid_f, 8, spread)

    @pl.when(has_prev)
    def _():
        swap(0, mid_f, tiles_f)

    add_x()
    chains(0)

    @pl.when(has_prev)
    def _():
        look_up(0, mid_f, tiles_f, table_f)
        deliver(0, mid_f, table_f, pick_f, act_out, 1, spread)
        deliver_own(0, mid_f, table_f, pick_f, act_out)

    @pl.when(s == 0)
    def _():
        clear(0, pick_f, act_out)

    @pl.when(has_prev)
    def _():
        relay(1, hop_b, mid_b, 1, spread)

    @pl.when(has_next)
    def _():
        swap(1, mid_b, tiles_b)

    @pl.when(has_next)
    def _():
        look_up(1, mid_b, tiles_b, table_b)
        deliver_own(1, mid_b, table_b, pick_b, grad_out)

    @pl.when(has_next)
    def _():
        deliver(1, mid_b, table_b, pick_b, grad_out, 1, 5)

    chains(1)

    @pl.when(has_next)
    def _():
        deliver(1, mid_b, table_b, pick_b, grad_out, 5, 9)

    chains(2)

    @pl.when(has_next)
    def _():
        deliver(1, mid_b, table_b, pick_b, grad_out, 9, 13)

    chains(3)

    @pl.when(has_next)
    def _():
        deliver(1, mid_b, table_b, pick_b, grad_out, 13, 16)

    @pl.when(s == sections - 1)
    def _():
        clear(1, pick_b, grad_out)


    arrived(chain_a.at[far_a - 1], a_recv.at[far_a - 1])
    total = piece[c, x, y] + chain_a[far_a - 1].astype(f32)
    if far_b:
        arrived(chain_b.at[far_b - 1], b_recv.at[far_b - 1])
        total = total + chain_b[far_b - 1].astype(f32)
    total = total * (1.0 / peers)
    final[...] = total
    final_gain[...] = jnp.sum(total[2 * share :, :share], axis=0, keepdims=True)
    stores = (
        pltpu.make_async_copy(final.at[pl.ds(0, share)], gdown_out, load_sem.at[0]),
        pltpu.make_async_copy(final.at[pl.ds(share, share)], gup_out, load_sem.at[1]),
        pltpu.make_async_copy(final_gain, ggain_out, load_sem.at[2]),
    )
    for store in stores:
        store.start()

    for k, half in enumerate((1 - x, x)):
        arrived(from_core.at[half], core_send.at[k])
    arrived(from_x, x_send)
    for t in range(far_a):
        arrived(chain_a.at[t], a_send.at[t])
    for t in range(far_b):
        arrived(chain_b.at[t], b_send.at[t])
    arrived(tiles_hop.at[pl.ds(0, spread - 1)], tile_send)

    for store in stores:
        store.wait()

    def settle_out(way, src):
        arrived(src.at[pl.ds(0, spread - 1)], p1_send.at[way])
        arrived(src, z_send.at[way])
        arrived(tiles_hop, tz_send.at[way])

    def settle_in(way, mid, tiles, pick, out):
        keep(way, pick, out, m).wait()
        arrived(half_of(mid, c), swap_send.at[way])
        arrived(tiles.at[c], tswap_send.at[way])
        arrived(pick.at[pl.ds(0, spread - 1)], p2_send.at[way])
        arrived(pick.at[pl.ds(0, spread - 1)], p2_recv.at[way])

    @pl.when(has_next)
    def _():
        settle_out(0, src_f)

    @pl.when(has_prev)
    def _():
        settle_out(1, src_b)

    @pl.when(has_prev)
    def _():
        settle_in(0, mid_f, tiles_f, pick_f, act_out)

    @pl.when(has_next)
    def _():
        settle_in(1, mid_b, tiles_b, pick_b, grad_out)


def place(*refs):
    count = (len(refs) - 2) // 3
    given, results, held = (refs[k * count : (k + 1) * count] for k in range(3))
    load_sem, store_sem = refs[-2:]
    loads = [pltpu.make_async_copy(given[k], held[k], load_sem.at[k]) for k in range(count)]
    stores = [pltpu.make_async_copy(held[k], results[k], store_sem.at[k]) for k in range(count)]
    for load in loads:
        load.start()
    for load, store in zip(loads, stores):
        load.wait()
        store.start()
    for store in stores:
        store.wait()


def on_device(sections, peers, acts, cotangent, gain, w_down, w_up, route_fwd, route_bwd, token_counts):
    batches, length, width = acts.shape[2:]
    units = w_up.shape[1]
    cap = batches + batches // 2
    rows = batches * length
    spread = peers // 2
    ring = spread // 2
    group = 16
    span = width // (spread // (length // group))
    share = width // peers
    height = 2 * share + group
    far_a, far_b = ring // 2, max(ring - 1 - ring // 2, 1)
    vmem, smem = pltpu.VMEM, pltpu.SMEM
    dma, pair = pltpu.SemaphoreType.DMA, pltpu.SemaphoreType.DMA((2,))
    in_hbm = pl.BlockSpec(memory_space=pltpu.HBM)
    mid = vmem((1 + 2 * spread * batches, group, span), bf16)
    pick = vmem((spread, cap, group, span), bf16)
    src = vmem((spread, batches, group, span), bf16)
    shapes = (
        jax.ShapeDtypeStruct((cap, length, width), bf16),
        jax.ShapeDtypeStruct((cap, length, width), bf16),
        jax.ShapeDtypeStruct((share, units), f32),
        jax.ShapeDtypeStruct((share, units), f32),
        jax.ShapeDtypeStruct((1, share), f32),
    )
    results = pl.pallas_call(
        functools.partial(kernel, sections, peers, cap),
        out_shape=shapes,
        in_specs=[in_hbm] * 8,
        out_specs=(in_hbm,) * 5,
        scratch_shapes=[
            smem((batches,), i32), smem((batches,), i32), smem((batches,), i32),
            vmem((rows, width), bf16), vmem((rows, width), bf16), vmem((1, width), f32),
            vmem((width, units), bf16), vmem((units, width), bf16),
            vmem((rows, width), bf16),
            vmem((rows, width), bf16),
            vmem((rows, width), f32),
            vmem((rows, 1), f32),
            vmem((group, width), f32),
            src, src, src, src, mid, mid, pick, pick,
            vmem((8, 128), i32), vmem((spread, 8, 128), i32),
            vmem((2, spread, 8, 128), i32), vmem((2, spread, 8, 128), i32),
            vmem((8, 128), i32), smem((8, 128), i32), smem((8, 128), i32),
            vmem((2, 2, ring, height, units), f32),
            vmem((2, ring, height, units), f32),
            vmem((ring, height, units), bf16), vmem((ring, height, units), bf16),
            vmem((far_a, height, units), bf16), vmem((far_b, height, units), bf16),
            vmem((far_a, height, units), bf16), vmem((far_b, height, units), bf16),
            vmem((height, units), f32), vmem((1, share), f32),
            pltpu.SemaphoreType.REGULAR, dma((2, spread)), dma((8,)), pair, dma((2, spread)), pair, dma((2, spread)), pair, pair,
            dma, dma, pair, pair, pair, pair,
            pair, pair, pair,
            pair, pair, dma, dma, dma((far_a,)), dma((far_a,)), dma((far_b,)), dma((far_b,)),
        ],
        compiler_params=pltpu.CompilerParams(
            collective_id=0, has_side_effects=True, vmem_limit_bytes=60 * 1024 * 1024
        ),
        cost_estimate=pl.CostEstimate(
            flops=12 * rows * width * units, bytes_accessed=8 * rows * width, transcendentals=rows * units
        ),
        name="adapter_relay",
    )(
        route_fwd.reshape(batches), route_bwd.reshape(batches), token_counts.reshape(batches),
        acts.reshape(rows, width), cotangent.reshape(rows, width), gain, w_down[0], w_up[0],
    )
    arrived_act, arrived_grad, grad_down, grad_up, grad_gain = pl.pallas_call(
        place,
        out_shape=shapes,
        in_specs=[in_hbm] * 5,
        out_specs=(in_hbm,) * 5,
        scratch_shapes=[vmem(made.shape, made.dtype) for made in shapes] + [dma((5,)), dma((5,))],
        compiler_params=pltpu.CompilerParams(vmem_limit_bytes=60 * 1024 * 1024),
        name="place_results",
    )(*results)
    return arrived_act[None, None], arrived_grad[None, None], grad_down[None], grad_up.T[None], grad_gain


def solution(mesh):
    placed = (
        P("section", "peer", None, None, None),
        P("section", "peer", None, None, None),
        P("section", None),
        P("section", None, None),
        P("section", None, None),
        P("section", "peer", None),
        P("section", "peer", None),
        P("section", "peer", None),
    )
    return jax.shard_map(
        functools.partial(on_device, mesh.shape["section"], mesh.shape["peer"]),
        mesh=mesh,
        in_specs=placed,
        out_specs=(
            P("section", "peer", None, None, None),
            P("section", "peer", None, None, None),
            P("section", "peer", None),
            P("section", None, "peer"),
            P("section", "peer"),
        ),
        check_vma=False,
    )
```

```python
import functools

import jax
import jax.numpy as jnp
from jax import lax
from jax.experimental import pallas as pl
from jax.experimental.pallas import tpu as pltpu
from jax.sharding import PartitionSpec as P

epsilon = 1e-05
MESH = pl.DeviceIdType.MESH
f32, bf16, i32 = jnp.float32, jnp.bfloat16, jnp.int32


def matmul(a, b, contract_a, contract_b):
    return lax.dot_general(
        a, b, (((contract_a,), (contract_b,)), ((), ())), preferred_element_type=f32
    )


def arrived(ref, sem):
    pltpu.make_async_copy(ref, ref, sem).wait()


def kernel(
    sections, peers, cap,
    fwd_hbm, bwd_hbm, counts_hbm, x_hbm, cot_hbm, gain_hbm, down_hbm, up_hbm,
    act_out, grad_out, gdown_out, gup_out, ggain_out,
    route_fwd, route_bwd, counts, x_ref, cot_ref, gain_ref, down_ref, up_ref,
    normed, masked, norm_grad, inverse, gain_acc,
    src_f, src_b, hop_f, hop_b, mid_f, mid_b, pick_f, pick_b,
    tile, tiles_hop, tiles_f, tiles_b, table_v, table_f, table_b,
    piece, from_core, sum_x, from_x, part_a, part_b, chain_a, chain_b, final, final_gain,
    hello, store_sem, load_sem, p1_send, p1_recv, z_send, z_recv, swap_send, swap_recv,
    tile_send, tile_recv, tz_send, tz_recv, tswap_send, tswap_recv,
    table_sem, p2_send, p2_recv,
    core_send, core_recv, x_send, x_recv, a_send, a_recv, b_send, b_recv,
):
    rows, width = x_ref.shape
    units = up_ref.shape[0]
    spread, batches, group, span = src_f.shape
    ring = spread // 2
    column_groups = width // span
    row_groups = spread // column_groups
    share = width // peers
    length = rows // batches

    s, p = lax.axis_index("section"), lax.axis_index("peer")
    c, m = p % 2, p // 2
    x, y = m % 2, m // 2
    sibling = p + 1 - 2 * c
    has_next = s < sections - 1
    has_prev = s > 0

    loads = [
        pltpu.make_async_copy(here, there, load_sem.at[k])
        for k, (here, there) in enumerate(
            (
                (x_hbm, x_ref), (gain_hbm, gain_ref), (down_hbm, down_ref), (up_hbm, up_ref),
                (counts_hbm, counts), (fwd_hbm, route_fwd), (bwd_hbm, route_bwd), (cot_hbm, cot_ref),
            )
        )
    ]
    for load in loads:
        load.start()

    def partner(i):
        k = i // 2
        odd = k % 2
        step = odd * ((k + 1) // 2) + (1 - odd) * (ring - k // 2)
        return ((y + step) % ring) * 2 + (x + i) % 2

    barrier = pltpu.get_barrier_semaphore()

    def greet(i, carry):
        pl.semaphore_signal(barrier, inc=1, device_id=(s, 2 * partner(i) + c), device_id_type=MESH)
        return carry

    lax.fori_loop(1, spread, greet, 0)
    pl.semaphore_signal(barrier, inc=1, device_id=(s, sibling), device_id_type=MESH)

    @pl.when(has_prev)
    def _():
        pl.semaphore_signal(barrier, inc=1, device_id=(s - 1, p), device_id_type=MESH)

    for load in loads[:7]:
        load.wait()
    row_ids = lax.broadcasted_iota(i32, (rows, 1), 0)
    limit = jnp.where(row_ids < length, counts[0], counts[1] + length)
    mask = (row_ids < limit).astype(f32)
    mask_small = mask.astype(bf16)

    def normalise(g, carry):
        here = pl.ds(pl.multiple_of(g * group, group), group)
        widened = x_ref[here, :].astype(f32)
        inv = lax.rsqrt(jnp.sum(widened * widened, axis=-1, keepdims=True) / width + epsilon)
        inverse[here, :] = inv
        normed[here, :] = (widened * inv * gain_ref[...]).astype(bf16)
        return carry

    lax.fori_loop(0, rows // group, normalise, 0, unroll=2)
    before = matmul(normed[...], down_ref[...], 1, 0)
    sig = jax.nn.sigmoid(before)
    active = (before * sig).astype(bf16)
    for k in range(column_groups):
        here = slice(k * span, (k + 1) * span)
        branch = matmul(active, up_ref[:, here], 1, 0)
        outputs = ((x_ref[:, here].astype(f32) + branch) * mask).astype(bf16)
        for g in range(rows // group):
            j, t = g // row_groups, g % row_groups
            src_f[t * column_groups + k, j] = outputs[g * group : (g + 1) * group]

    kinds = lax.broadcasted_iota(i32, tile.shape, 0)
    routes = jnp.where(
        kinds < 2,
        jnp.where(kinds == 0, route_fwd[0], route_fwd[1]),
        jnp.where(kinds == 2, route_bwd[0], route_bwd[1]),
    )
    tile[...] = routes
    tiles_hop[m] = routes

    pl.semaphore_wait(barrier, spread + has_next.astype(i32))

    @pl.when(has_next)
    def _():
        pl.semaphore_signal(hello, inc=1, device_id=(s + 1, p), device_id_type=MESH)

    def send_tile(i, carry):
        pltpu.make_async_remote_copy(
            src_ref=tile, dst_ref=tiles_hop.at[m], send_sem=tile_send, recv_sem=tile_recv,
            device_id=(s, 2 * partner(i) + c), device_id_type=MESH,
        ).start()
        return carry

    lax.fori_loop(1, spread, send_tile, 0)

    def slots(origin):
        return pl.ds(1 + (c * spread + origin) * batches, batches)

    def shift(way, chunk, origin, mid):
        pltpu.make_async_remote_copy(
            src_ref=chunk, dst_ref=mid.at[slots(origin)],
            send_sem=z_send.at[way], recv_sem=z_recv.at[way, origin],
            device_id=(s + 1 - 2 * way, p), device_id_type=MESH,
        ).start()

    def spread_out(way, src, hop):
        def step(i, carry):
            to = partner(i)
            pltpu.make_async_remote_copy(
                src_ref=src.at[to], dst_ref=hop.at[m],
                send_sem=p1_send.at[way], recv_sem=p1_recv.at[way, m],
                device_id=(s, 2 * to + c), device_id_type=MESH,
            ).start()
            return carry

        lax.fori_loop(1, spread, step, 0)

    def relay(way, hop, mid, first, last):
        def step(i, carry):
            origin = partner(i)
            arrived(hop.at[origin], p1_recv.at[way, origin])
            shift(way, hop.at[origin], origin, mid)
            return carry

        lax.fori_loop(first, last, step, 0)

    @pl.when(has_next)
    def _():
        spread_out(0, src_f, hop_f)
        shift(0, src_f.at[m], m, mid_f)

    loads[7].wait()
    masked[...] = cot_ref[...] * mask_small
    act_grad = matmul(masked[...], up_ref[...], 1, 1)
    pre_grad = (act_grad * sig * (1.0 + before * (1.0 - sig))).astype(bf16)
    for k in range(column_groups):
        here = slice(k * span, (k + 1) * span)
        norm_grad[:, here] = matmul(pre_grad, down_ref[here, :], 1, 1)
    gain_acc[...] = jnp.zeros_like(gain_acc)

    def input_grad(g, carry):
        here = pl.ds(pl.multiple_of(g * group, group), group)
        inv = inverse[here, :]
        unit = x_ref[here, :].astype(f32) * inv
        ng = norm_grad[here, :]
        product = ng * unit
        gain_acc[...] += product
        scaled = ng * gain_ref[...]
        mean = jnp.sum(scaled * unit, axis=-1, keepdims=True) / width
        grad = (masked[here, :].astype(f32) + inv * (scaled - unit * mean)).astype(bf16)
        for k in range(column_groups):
            src_b[(g % row_groups) * column_groups + k, g // row_groups] = grad[
                :, k * span : (k + 1) * span
            ]
        return carry

    lax.fori_loop(0, rows // group, input_grad, 0)

    per_group = span // share
    for k in range(column_groups):
        here = slice(k * span, (k + 1) * span)
        down_part = matmul(normed[:, here], pre_grad, 0, 0)
        up_part = matmul(masked[:, here], active, 0, 0)
        for i in range(per_group):
            q = k * per_group + i
            own = (q % 2, (q // 2) % 2, q // 4)
            mine = slice(i * share, (i + 1) * share)
            piece[own + (slice(0, share),)] = down_part[mine]
            piece[own + (slice(share, 2 * share),)] = up_part[mine]
            gains = gain_acc[:, q * share : (q + 1) * share]
            blank = jnp.zeros((gains.shape[0], units - share), f32)
            piece[own + (slice(2 * share, 2 * share + group),)] = jnp.concatenate([gains, blank], axis=1)

    def to_core(k, half):
        return pltpu.make_async_remote_copy(
            src_ref=piece.at[1 - c, half], dst_ref=from_core.at[half],
            send_sem=core_send.at[k], recv_sem=core_recv.at[k],
            device_id=(s, sibling), device_id_type=MESH,
        )

    to_core(0, 1 - x).start()
    to_core(1, x).start()

    @pl.when(has_next)
    def _():
        relay(0, hop_f, mid_f, 1, spread // 2)

    @pl.when(has_prev)
    def _():
        spread_out(1, src_b, hop_b)

    def add_core(k, half):
        arrived(from_core.at[half], core_recv.at[k])

        def step(i, carry):
            total = piece[c, half, i] + from_core[half, i]
            if k == 0:
                sum_x[i] = total.astype(bf16)
            else:
                piece[c, half, i] = total
            return carry

        lax.fori_loop(0, ring, step, 0)

    add_core(0, 1 - x)
    to_x = pltpu.make_async_remote_copy(
        src_ref=sum_x, dst_ref=from_x,
        send_sem=x_send, recv_sem=x_recv,
        device_id=(s, 2 * (m + 1 - 2 * x) + c), device_id_type=MESH,
    )
    to_x.start()
    add_core(1, x)

    arrived(tiles_hop.at[pl.ds(0, spread - 1)], tile_recv)

    def shift_tiles(way, tiles):
        pltpu.make_async_remote_copy(
            src_ref=tiles_hop, dst_ref=tiles.at[c],
            send_sem=tz_send.at[way], recv_sem=tz_recv.at[way],
            device_id=(s + 1 - 2 * way, p), device_id_type=MESH,
        ).start()

    @pl.when(has_next)
    def _():
        shift_tiles(0, tiles_f)

    @pl.when(has_prev)
    def _():
        pl.semaphore_wait(hello, 1)
        shift_tiles(1, tiles_b)
        shift(1, src_b.at[m], m, mid_b)

    def swap(way, mid, tiles):
        def step(i, carry):
            origin = partner(i)
            here = mid.at[slots(origin)]
            arrived(here, z_recv.at[way, origin])
            pltpu.make_async_remote_copy(
                src_ref=here, dst_ref=here,
                send_sem=swap_send.at[way], recv_sem=swap_recv.at[way],
                device_id=(s, sibling), device_id_type=MESH,
            ).start()
            return carry

        lax.fori_loop(0, spread, step, 0)
        arrived(tiles.at[c], tz_recv.at[way])
        pltpu.make_async_remote_copy(
            src_ref=tiles.at[c], dst_ref=tiles.at[c],
            send_sem=tswap_send.at[way], recv_sem=tswap_recv.at[way],
            device_id=(s, sibling), device_id_type=MESH,
        ).start()

    def chunk_of(out, k):
        tokens = pl.ds(pl.multiple_of((k // column_groups) * group, group), group)
        columns = pl.ds(pl.multiple_of((k % column_groups) * span, 128), span)
        return out.at[:, tokens, columns]

    def keep(way, pick, out, k):
        return pltpu.make_async_copy(pick.at[k], chunk_of(out, k), store_sem.at[way, k])

    def half_of(mid, core):
        return mid.at[pl.ds(1 + core * spread * batches, spread * batches)]

    def look_up(way, mid, tiles, table):
        arrived(tiles.at[1 - c], tswap_recv.at[way])
        lanes = lax.broadcasted_iota(i32, (1, tiles.shape[3]), 1)

        def count(i, carry):
            seen, chosen = carry
            for core in range(2):
                for j in range(batches):
                    at = way * batches + j
                    hit = tiles[core, i, at : at + 1, :] == lanes
                    name = 1 + (core * spread + i) * batches + j
                    chosen = tuple(
                        old + jnp.where(hit & (seen == k), name, 0) for k, old in enumerate(chosen)
                    )
                    seen = seen + hit.astype(i32)
            return seen, chosen

        table_v[...] = jnp.zeros_like(table_v)
        none = jnp.zeros_like(lanes)
        _, chosen = lax.fori_loop(0, spread, count, (none, (none,) * cap))
        for k in range(cap):
            table_v[k : k + 1, :] = chosen[k]
        to_table = pltpu.make_async_copy(table_v, table, table_sem.at[way])
        to_table.start()
        mid[0] = jnp.zeros(mid.shape[1:], bf16)
        to_table.wait()
        arrived(half_of(mid, 1 - c), swap_recv.at[way])

    def deliver(way, mid, table, pick, out, first, last):
        def step(i, carry):
            to = partner(spread - i)
            for k in range(cap):
                pick[to, k] = mid[table[k, 2 * to + c]]
            pltpu.make_async_remote_copy(
                src_ref=pick.at[to], dst_ref=chunk_of(out, m),
                send_sem=p2_send.at[way], recv_sem=p2_recv.at[way],
                device_id=(s, 2 * to + c), device_id_type=MESH,
            ).start()
            return carry

        lax.fori_loop(first, last, step, 0)

    def deliver_own(way, mid, table, pick, out):
        for k in range(cap):
            pick[m, k] = mid[table[k, p]]
        keep(way, pick, out, m).start()

    def clear(way, pick, out):
        def fill(k, carry):
            pick[k] = jnp.zeros(pick.shape[1:], bf16)
            keep(way, pick, out, k).start()
            return carry

        def finish(k, carry):
            keep(way, pick, out, k).wait()
            return carry

        lax.fori_loop(0, spread, fill, 0)
        lax.fori_loop(0, spread, finish, 0)

    turn = 1 - 2 * c
    far_a, far_b = ring // 2, ring - 1 - ring // 2

    def along(step):
        return (y + ring + step) % ring

    def chain_step(t, far, way, part, hold, send, recv):
        total = piece[c, x, along(way * (far - t))]
        if t > 0:
            arrived(hold.at[t - 1], recv.at[t - 1])
            total = total + hold[t - 1].astype(f32)
        part[t] = total.astype(bf16)
        pltpu.make_async_remote_copy(
            src_ref=part.at[t], dst_ref=hold.at[t],
            send_sem=send.at[t], recv_sem=recv.at[t],
            device_id=(s, 4 * along(way) + 2 * x + c), device_id_type=MESH,
        ).start()

    def chains(t):
        if t < far_a:
            chain_step(t, far_a, turn, part_a, chain_a, a_send, a_recv)
        if t < far_b:
            chain_step(t, far_b, -turn, part_b, chain_b, b_send, b_recv)

    def add_x():
        arrived(from_x, x_recv)

        def step(i, carry):
            piece[c, x, i] += from_x[i].astype(f32)
            return carry

        lax.fori_loop(0, ring, step, 0)

    quarter = spread // 4

    @pl.when(has_next)
    def _():
        relay(0, hop_f, mid_f, spread // 2, spread)

    @pl.when(has_prev)
    def _():
        swap(0, mid_f, tiles_f)

    add_x()
    chains(0)

    @pl.when(has_prev)
    def _():
        look_up(0, mid_f, tiles_f, table_f)
        deliver(0, mid_f, table_f, pick_f, act_out, 1, spread)
        deliver_own(0, mid_f, table_f, pick_f, act_out)

    @pl.when(s == 0)
    def _():
        clear(0, pick_f, act_out)

    @pl.when(has_prev)
    def _():
        relay(1, hop_b, mid_b, 1, spread)

    @pl.when(has_next)
    def _():
        swap(1, mid_b, tiles_b)

    @pl.when(has_next)
    def _():
        look_up(1, mid_b, tiles_b, table_b)
        deliver_own(1, mid_b, table_b, pick_b, grad_out)

    @pl.when(has_next)
    def _():
        deliver(1, mid_b, table_b, pick_b, grad_out, 1, 1 + quarter)

    chains(1)

    @pl.when(has_next)
    def _():
        deliver(1, mid_b, table_b, pick_b, grad_out, 1 + quarter, 1 + 2 * quarter)

    chains(2)

    @pl.when(has_next)
    def _():
        deliver(1, mid_b, table_b, pick_b, grad_out, 1 + 2 * quarter, 1 + 3 * quarter)

    chains(3)

    @pl.when(has_next)
    def _():
        deliver(1, mid_b, table_b, pick_b, grad_out, 1 + 3 * quarter, spread)

    @pl.when(s == sections - 1)
    def _():
        clear(1, pick_b, grad_out)


    arrived(chain_a.at[far_a - 1], a_recv.at[far_a - 1])
    total = piece[c, x, y] + chain_a[far_a - 1].astype(f32)
    if far_b:
        arrived(chain_b.at[far_b - 1], b_recv.at[far_b - 1])
        total = total + chain_b[far_b - 1].astype(f32)
    total = total * (1.0 / peers)
    final[...] = total
    final_gain[...] = jnp.sum(total[2 * share :, :share], axis=0, keepdims=True)
    stores = (
        pltpu.make_async_copy(final.at[pl.ds(0, share)], gdown_out, load_sem.at[0]),
        pltpu.make_async_copy(final.at[pl.ds(share, share)], gup_out, load_sem.at[1]),
        pltpu.make_async_copy(final_gain, ggain_out, load_sem.at[2]),
    )
    for store in stores:
        store.start()

    for k, half in enumerate((1 - x, x)):
        arrived(from_core.at[half], core_send.at[k])
    arrived(from_x, x_send)
    for t in range(far_a):
        arrived(chain_a.at[t], a_send.at[t])
    for t in range(far_b):
        arrived(chain_b.at[t], b_send.at[t])
    arrived(tiles_hop.at[pl.ds(0, spread - 1)], tile_send)

    for store in stores:
        store.wait()

    def settle_out(way, src):
        arrived(src.at[pl.ds(0, spread - 1)], p1_send.at[way])
        arrived(src, z_send.at[way])
        arrived(tiles_hop, tz_send.at[way])

    def settle_in(way, mid, tiles, pick, out):
        keep(way, pick, out, m).wait()
        arrived(half_of(mid, c), swap_send.at[way])
        arrived(tiles.at[c], tswap_send.at[way])
        arrived(pick.at[pl.ds(0, spread - 1)], p2_send.at[way])
        arrived(pick.at[pl.ds(0, spread - 1)], p2_recv.at[way])

    @pl.when(has_next)
    def _():
        settle_out(0, src_f)

    @pl.when(has_prev)
    def _():
        settle_out(1, src_b)

    @pl.when(has_prev)
    def _():
        settle_in(0, mid_f, tiles_f, pick_f, act_out)

    @pl.when(has_next)
    def _():
        settle_in(1, mid_b, tiles_b, pick_b, grad_out)


def place(*refs):
    count = (len(refs) - 2) // 3
    given, results, held = (refs[k * count : (k + 1) * count] for k in range(3))
    load_sem, store_sem = refs[-2:]
    slots = given[0].shape[0]
    parts = [(k, pl.ds(i, 1)) for i in range(slots) for k in (0, 1)]
    parts += [(k, slice(None)) for k in range(2, count)]
    loads, stores = [], []
    for n, (k, cut) in enumerate(parts):
        loads.append(pltpu.make_async_copy(given[k].at[cut], held[k].at[cut], load_sem.at[n]))
        stores.append(pltpu.make_async_copy(held[k].at[cut], results[k].at[cut], store_sem.at[n]))
    for load in loads:
        load.start()
    for load, store in zip(loads, stores):
        load.wait()
        store.start()
    for store in stores:
        store.wait()


def on_device(sections, peers, acts, cotangent, gain, w_down, w_up, route_fwd, route_bwd, token_counts):
    batches, length, width = acts.shape[2:]
    units = w_up.shape[1]
    cap = batches + batches // 2
    rows = batches * length
    spread = peers // 2
    ring = spread // 2
    group = 16
    span = width // (spread // (length // group))
    share = width // peers
    height = 2 * share + group
    far_a, far_b = ring // 2, max(ring - 1 - ring // 2, 1)
    vmem, smem = pltpu.VMEM, pltpu.SMEM
    dma, pair = pltpu.SemaphoreType.DMA, pltpu.SemaphoreType.DMA((2,))
    in_hbm = pl.BlockSpec(memory_space=pltpu.HBM)
    mid = vmem((1 + 2 * spread * batches, group, span), bf16)
    pick = vmem((spread, cap, group, span), bf16)
    src = vmem((spread, batches, group, span), bf16)
    shapes = (
        jax.ShapeDtypeStruct((cap, length, width), bf16),
        jax.ShapeDtypeStruct((cap, length, width), bf16),
        jax.ShapeDtypeStruct((share, units), f32),
        jax.ShapeDtypeStruct((share, units), f32),
        jax.ShapeDtypeStruct((1, share), f32),
    )
    results = pl.pallas_call(
        functools.partial(kernel, sections, peers, cap),
        out_shape=shapes,
        in_specs=[in_hbm] * 8,
        out_specs=(in_hbm,) * 5,
        scratch_shapes=[
            smem((batches,), i32), smem((batches,), i32), smem((batches,), i32),
            vmem((rows, width), bf16), vmem((rows, width), bf16), vmem((1, width), f32),
            vmem((width, units), bf16), vmem((units, width), bf16),
            vmem((rows, width), bf16),
            vmem((rows, width), bf16),
            vmem((rows, width), f32),
            vmem((rows, 1), f32),
            vmem((group, width), f32),
            src, src, src, src, mid, mid, pick, pick,
            vmem((8, 128), i32), vmem((spread, 8, 128), i32),
            vmem((2, spread, 8, 128), i32), vmem((2, spread, 8, 128), i32),
            vmem((8, 128), i32), smem((8, 128), i32), smem((8, 128), i32),
            vmem((2, 2, ring, height, units), f32),
            vmem((2, ring, height, units), f32),
            vmem((ring, height, units), bf16), vmem((ring, height, units), bf16),
            vmem((far_a, height, units), bf16), vmem((far_b, height, units), bf16),
            vmem((far_a, height, units), bf16), vmem((far_b, height, units), bf16),
            vmem((height, units), f32), vmem((1, share), f32),
            pltpu.SemaphoreType.REGULAR, dma((2, spread)), dma((8,)), pair, dma((2, spread)), pair, dma((2, spread)), pair, pair,
            dma, dma, pair, pair, pair, pair,
            pair, pair, pair,
            pair, pair, dma, dma, dma((far_a,)), dma((far_a,)), dma((far_b,)), dma((far_b,)),
        ],
        compiler_params=pltpu.CompilerParams(
            collective_id=0, has_side_effects=True, vmem_limit_bytes=60 * 1024 * 1024
        ),
        cost_estimate=pl.CostEstimate(
            flops=12 * rows * width * units, bytes_accessed=8 * rows * width, transcendentals=rows * units
        ),
        name="adapter_relay",
    )(
        route_fwd.reshape(batches), route_bwd.reshape(batches), token_counts.reshape(batches),
        acts.reshape(rows, width), cotangent.reshape(rows, width), gain, w_down[0], w_up[0],
    )
    arrived_act, arrived_grad, grad_down, grad_up, grad_gain = pl.pallas_call(
        place,
        out_shape=shapes,
        in_specs=[in_hbm] * 5,
        out_specs=(in_hbm,) * 5,
        scratch_shapes=[vmem(made.shape, made.dtype) for made in shapes] + [dma((2 * cap + 3,)), dma((2 * cap + 3,))],
        compiler_params=pltpu.CompilerParams(vmem_limit_bytes=60 * 1024 * 1024),
        name="place_results",
    )(*results)
    return arrived_act[None, None], arrived_grad[None, None], grad_down[None], grad_up.T[None], grad_gain


def solution(mesh):
    placed = (
        P("section", "peer", None, None, None),
        P("section", "peer", None, None, None),
        P("section", None),
        P("section", None, None),
        P("section", None, None),
        P("section", "peer", None),
        P("section", "peer", None),
        P("section", "peer", None),
    )
    return jax.shard_map(
        functools.partial(on_device, mesh.shape["section"], mesh.shape["peer"]),
        mesh=mesh,
        in_specs=placed,
        out_specs=(
            P("section", "peer", None, None, None),
            P("section", "peer", None, None, None),
            P("section", "peer", None),
            P("section", None, "peer"),
            P("section", "peer"),
        ),
        check_vma=False,
    )
```

```python
import functools

import jax
import jax.numpy as jnp
from jax import lax
from jax.experimental import pallas as pl
from jax.experimental.pallas import tpu as pltpu
from jax.sharding import PartitionSpec as P

epsilon = 1e-05
MESH = pl.DeviceIdType.MESH
f32, bf16, i32 = jnp.float32, jnp.bfloat16, jnp.int32


def matmul(a, b, contract_a, contract_b):
    return lax.dot_general(
        a, b, (((contract_a,), (contract_b,)), ((), ())), preferred_element_type=f32
    )


def arrived(ref, sem):
    pltpu.make_async_copy(ref, ref, sem).wait()


def kernel(
    sections, peers, cap,
    fwd_hbm, bwd_hbm, counts_hbm, x_hbm, cot_hbm, gain_hbm, down_hbm, up_hbm,
    act_out, grad_out, gdown_out, gup_out, ggain_out,
    route_fwd, route_bwd, counts, x_ref, cot_ref, gain_ref, down_ref, up_ref,
    normed, masked, norm_grad, inverse, gain_acc,
    src_f, src_b, hop_f, hop_b, mid_f, mid_b, pick_f, pick_b,
    tile, tiles_hop, tiles_f, tiles_b, table_v, table_f, table_b,
    piece, from_core, sum_x, from_x, part_a, part_b, chain_a, chain_b, final, final_gain,
    hello, store_sem, load_sem, p1_send, p1_recv, z_send, z_recv, swap_send, swap_recv,
    tile_send, tile_recv, tz_send, tz_recv, tswap_send, tswap_recv,
    table_sem, p2_send, p2_recv,
    core_send, core_recv, x_send, x_recv, a_send, a_recv, b_send, b_recv,
):
    rows, width = x_ref.shape
    units = up_ref.shape[0]
    spread, batches, group, span = src_f.shape
    ring = spread // 2
    column_groups = width // span
    row_groups = spread // column_groups
    share = width // peers
    length = rows // batches

    s, p = lax.axis_index("section"), lax.axis_index("peer")
    c, m = p % 2, p // 2
    x, y = m % 2, m // 2
    sibling = p + 1 - 2 * c
    has_next = s < sections - 1
    has_prev = s > 0

    loads = [
        pltpu.make_async_copy(here, there, load_sem.at[k])
        for k, (here, there) in enumerate(
            (
                (x_hbm, x_ref), (gain_hbm, gain_ref), (down_hbm, down_ref), (up_hbm, up_ref),
                (counts_hbm, counts), (fwd_hbm, route_fwd), (bwd_hbm, route_bwd), (cot_hbm, cot_ref),
            )
        )
    ]
    for load in loads:
        load.start()

    def partner(i):
        k = i // 2
        odd = k % 2
        step = odd * ((k + 1) // 2) + (1 - odd) * (ring - k // 2)
        return ((y + step) % ring) * 2 + (x + i) % 2

    barrier = pltpu.get_barrier_semaphore()

    def greet(i, carry):
        pl.semaphore_signal(barrier, inc=1, device_id=(s, 2 * partner(i) + c), device_id_type=MESH)
        return carry

    lax.fori_loop(1, spread, greet, 0)
    pl.semaphore_signal(barrier, inc=1, device_id=(s, sibling), device_id_type=MESH)

    @pl.when(has_prev)
    def _():
        pl.semaphore_signal(barrier, inc=1, device_id=(s - 1, p), device_id_type=MESH)

    for load in loads[:7]:
        load.wait()
    row_ids = lax.broadcasted_iota(i32, (rows, 1), 0)
    limit = jnp.where(row_ids < length, counts[0], counts[1] + length)
    mask = (row_ids < limit).astype(f32)
    mask_small = mask.astype(bf16)

    def normalise(g, carry):
        here = pl.ds(pl.multiple_of(g * group, group), group)
        widened = x_ref[here, :].astype(f32)
        inv = lax.rsqrt(jnp.sum(widened * widened, axis=-1, keepdims=True) / width + epsilon)
        inverse[here, :] = inv
        normed[here, :] = (widened * inv * gain_ref[...]).astype(bf16)
        return carry

    lax.fori_loop(0, rows // group, normalise, 0, unroll=2)
    before = matmul(normed[...], down_ref[...], 1, 0)
    sig = jax.nn.sigmoid(before)
    active = (before * sig).astype(bf16)
    for k in range(column_groups):
        here = slice(k * span, (k + 1) * span)
        branch = matmul(active, up_ref[:, here], 1, 0)
        outputs = ((x_ref[:, here].astype(f32) + branch) * mask).astype(bf16)
        for g in range(rows // group):
            j, t = g // row_groups, g % row_groups
            src_f[t * column_groups + k, j] = outputs[g * group : (g + 1) * group]

    kinds = lax.broadcasted_iota(i32, tile.shape, 0)
    routes = jnp.where(
        kinds < 2,
        jnp.where(kinds == 0, route_fwd[0], route_fwd[1]),
        jnp.where(kinds == 2, route_bwd[0], route_bwd[1]),
    )
    tile[...] = routes
    tiles_hop[m] = routes

    pl.semaphore_wait(barrier, spread + has_next.astype(i32))

    @pl.when(has_next)
    def _():
        pl.semaphore_signal(hello, inc=1, device_id=(s + 1, p), device_id_type=MESH)

    def send_tile(i, carry):
        pltpu.make_async_remote_copy(
            src_ref=tile, dst_ref=tiles_hop.at[m], send_sem=tile_send, recv_sem=tile_recv,
            device_id=(s, 2 * partner(i) + c), device_id_type=MESH,
        ).start()
        return carry

    lax.fori_loop(1, spread, send_tile, 0)

    def slots(origin):
        return pl.ds(1 + (c * spread + origin) * batches, batches)

    def shift(way, chunk, origin, mid):
        pltpu.make_async_remote_copy(
            src_ref=chunk, dst_ref=mid.at[slots(origin)],
            send_sem=z_send.at[way], recv_sem=z_recv.at[way, origin],
            device_id=(s + 1 - 2 * way, p), device_id_type=MESH,
        ).start()

    def spread_out(way, src, hop):
        def step(i, carry):
            to = partner(i)
            pltpu.make_async_remote_copy(
                src_ref=src.at[to], dst_ref=hop.at[m],
                send_sem=p1_send.at[way], recv_sem=p1_recv.at[way, m],
                device_id=(s, 2 * to + c), device_id_type=MESH,
            ).start()
            return carry

        lax.fori_loop(1, spread, step, 0)

    def relay(way, hop, mid, first, last):
        def step(i, carry):
            origin = partner(i)
            arrived(hop.at[origin], p1_recv.at[way, origin])
            shift(way, hop.at[origin], origin, mid)
            return carry

        lax.fori_loop(first, last, step, 0)

    @pl.when(has_next)
    def _():
        spread_out(0, src_f, hop_f)
        shift(0, src_f.at[m], m, mid_f)

    loads[7].wait()
    masked[...] = cot_ref[...] * mask_small
    act_grad = matmul(masked[...], up_ref[...], 1, 1)
    pre_grad = (act_grad * sig * (1.0 + before * (1.0 - sig))).astype(bf16)
    for k in range(column_groups):
        here = slice(k * span, (k + 1) * span)
        norm_grad[:, here] = matmul(pre_grad, down_ref[here, :], 1, 1)
    gain_acc[...] = jnp.zeros_like(gain_acc)

    def input_grad(g, carry):
        here = pl.ds(pl.multiple_of(g * group, group), group)
        inv = inverse[here, :]
        unit = x_ref[here, :].astype(f32) * inv
        ng = norm_grad[here, :]
        product = ng * unit
        gain_acc[...] += product
        scaled = ng * gain_ref[...]
        mean = jnp.sum(scaled * unit, axis=-1, keepdims=True) / width
        grad = (masked[here, :].astype(f32) + inv * (scaled - unit * mean)).astype(bf16)
        for k in range(column_groups):
            src_b[(g % row_groups) * column_groups + k, g // row_groups] = grad[
                :, k * span : (k + 1) * span
            ]
        return carry

    lax.fori_loop(0, rows // group, input_grad, 0)

    per_group = span // share
    for k in range(column_groups):
        here = slice(k * span, (k + 1) * span)
        down_part = matmul(normed[:, here], pre_grad, 0, 0)
        up_part = matmul(masked[:, here], active, 0, 0)
        for i in range(per_group):
            q = k * per_group + i
            own = (q % 2, (q // 2) % 2, q // 4)
            mine = slice(i * share, (i + 1) * share)
            piece[own + (slice(0, share),)] = down_part[mine]
            piece[own + (slice(share, 2 * share),)] = up_part[mine]
            gains = gain_acc[:, q * share : (q + 1) * share]
            blank = jnp.zeros((gains.shape[0], units - share), f32)
            piece[own + (slice(2 * share, 2 * share + group),)] = jnp.concatenate([gains, blank], axis=1)

    def to_core(k, half):
        return pltpu.make_async_remote_copy(
            src_ref=piece.at[1 - c, half], dst_ref=from_core.at[half],
            send_sem=core_send.at[k], recv_sem=core_recv.at[k],
            device_id=(s, sibling), device_id_type=MESH,
        )

    to_core(0, 1 - x).start()
    to_core(1, x).start()

    @pl.when(has_next)
    def _():
        relay(0, hop_f, mid_f, 1, spread // 2)

    @pl.when(has_prev)
    def _():
        spread_out(1, src_b, hop_b)

    def add_core(k, half):
        arrived(from_core.at[half], core_recv.at[k])

        def step(i, carry):
            total = piece[c, half, i] + from_core[half, i]
            if k == 0:
                sum_x[i] = total.astype(bf16)
            else:
                piece[c, half, i] = total
            return carry

        lax.fori_loop(0, ring, step, 0)

    add_core(0, 1 - x)
    to_x = pltpu.make_async_remote_copy(
        src_ref=sum_x, dst_ref=from_x,
        send_sem=x_send, recv_sem=x_recv,
        device_id=(s, 2 * (m + 1 - 2 * x) + c), device_id_type=MESH,
    )
    to_x.start()
    add_core(1, x)

    arrived(tiles_hop.at[pl.ds(0, spread - 1)], tile_recv)

    def shift_tiles(way, tiles):
        pltpu.make_async_remote_copy(
            src_ref=tiles_hop, dst_ref=tiles.at[c],
            send_sem=tz_send.at[way], recv_sem=tz_recv.at[way],
            device_id=(s + 1 - 2 * way, p), device_id_type=MESH,
        ).start()

    @pl.when(has_next)
    def _():
        shift_tiles(0, tiles_f)

    @pl.when(has_prev)
    def _():
        pl.semaphore_wait(hello, 1)
        shift_tiles(1, tiles_b)
        shift(1, src_b.at[m], m, mid_b)

    def swap(way, mid, tiles):
        def step(i, carry):
            origin = partner(i)
            here = mid.at[slots(origin)]
            arrived(here, z_recv.at[way, origin])
            pltpu.make_async_remote_copy(
                src_ref=here, dst_ref=here,
                send_sem=swap_send.at[way], recv_sem=swap_recv.at[way],
                device_id=(s, sibling), device_id_type=MESH,
            ).start()
            return carry

        lax.fori_loop(0, spread, step, 0)
        arrived(tiles.at[c], tz_recv.at[way])
        pltpu.make_async_remote_copy(
            src_ref=tiles.at[c], dst_ref=tiles.at[c],
            send_sem=tswap_send.at[way], recv_sem=tswap_recv.at[way],
            device_id=(s, sibling), device_id_type=MESH,
        ).start()

    def chunk_of(out, k):
        tokens = pl.ds(pl.multiple_of((k // column_groups) * group, group), group)
        columns = pl.ds(pl.multiple_of((k % column_groups) * span, 128), span)
        return out.at[:, tokens, columns]

    def keep(way, pick, out, k):
        return pltpu.make_async_copy(pick.at[k], chunk_of(out, k), store_sem.at[way, k])

    def half_of(mid, core):
        return mid.at[pl.ds(1 + core * spread * batches, spread * batches)]

    def look_up(way, mid, tiles, table):
        arrived(tiles.at[1 - c], tswap_recv.at[way])
        lanes = lax.broadcasted_iota(i32, (1, tiles.shape[3]), 1)

        def count(i, carry):
            seen, chosen = carry
            for core in range(2):
                for j in range(batches):
                    at = way * batches + j
                    hit = tiles[core, i, at : at + 1, :] == lanes
                    name = 1 + (core * spread + i) * batches + j
                    chosen = tuple(
                        old + jnp.where(hit & (seen == k), name, 0) for k, old in enumerate(chosen)
                    )
                    seen = seen + hit.astype(i32)
            return seen, chosen

        table_v[...] = jnp.zeros_like(table_v)
        none = jnp.zeros_like(lanes)
        _, chosen = lax.fori_loop(0, spread, count, (none, (none,) * cap))
        for k in range(cap):
            table_v[k : k + 1, :] = chosen[k]
        to_table = pltpu.make_async_copy(table_v, table, table_sem.at[way])
        to_table.start()
        mid[0] = jnp.zeros(mid.shape[1:], bf16)
        to_table.wait()
        arrived(half_of(mid, 1 - c), swap_recv.at[way])

    def deliver(way, mid, table, pick, out, first, last):
        def step(i, carry):
            to = partner(spread - i)
            for k in range(cap):
                pick[to, k] = mid[table[k, 2 * to + c]]
            pltpu.make_async_remote_copy(
                src_ref=pick.at[to], dst_ref=chunk_of(out, m),
                send_sem=p2_send.at[way], recv_sem=p2_recv.at[way],
                device_id=(s, 2 * to + c), device_id_type=MESH,
            ).start()
            return carry

        lax.fori_loop(first, last, step, 0)

    def deliver_own(way, mid, table, pick, out):
        for k in range(cap):
            pick[m, k] = mid[table[k, p]]
        keep(way, pick, out, m).start()

    def clear(way, pick, out):
        def fill(k, carry):
            pick[k] = jnp.zeros(pick.shape[1:], bf16)
            keep(way, pick, out, k).start()
            return carry

        def finish(k, carry):
            keep(way, pick, out, k).wait()
            return carry

        lax.fori_loop(0, spread, fill, 0)
        lax.fori_loop(0, spread, finish, 0)

    turn = 1 - 2 * c
    far_a, far_b = ring // 2, ring - 1 - ring // 2

    def along(step):
        return (y + ring + step) % ring

    def chain_step(t, far, way, part, hold, send, recv):
        total = piece[c, x, along(way * (far - t))]
        if t > 0:
            arrived(hold.at[t - 1], recv.at[t - 1])
            total = total + hold[t - 1].astype(f32)
        part[t] = total.astype(bf16)
        pltpu.make_async_remote_copy(
            src_ref=part.at[t], dst_ref=hold.at[t],
            send_sem=send.at[t], recv_sem=recv.at[t],
            device_id=(s, 4 * along(way) + 2 * x + c), device_id_type=MESH,
        ).start()

    def chains(t):
        if t < far_a:
            chain_step(t, far_a, turn, part_a, chain_a, a_send, a_recv)
        if t < far_b:
            chain_step(t, far_b, -turn, part_b, chain_b, b_send, b_recv)

    def add_x():
        arrived(from_x, x_recv)

        def step(i, carry):
            piece[c, x, i] += from_x[i].astype(f32)
            return carry

        lax.fori_loop(0, ring, step, 0)

    quarter = spread // 4

    @pl.when(has_next)
    def _():
        relay(0, hop_f, mid_f, spread // 2, spread)

    @pl.when(has_prev)
    def _():
        swap(0, mid_f, tiles_f)

    add_x()
    chains(0)

    @pl.when(has_prev)
    def _():
        look_up(0, mid_f, tiles_f, table_f)
        deliver(0, mid_f, table_f, pick_f, act_out, 1, spread)
        deliver_own(0, mid_f, table_f, pick_f, act_out)

    @pl.when(s == 0)
    def _():
        clear(0, pick_f, act_out)

    @pl.when(has_prev)
    def _():
        relay(1, hop_b, mid_b, 1, spread)

    @pl.when(has_next)
    def _():
        swap(1, mid_b, tiles_b)

    chains(1)

    @pl.when(has_next)
    def _():
        look_up(1, mid_b, tiles_b, table_b)
        deliver_own(1, mid_b, table_b, pick_b, grad_out)

    @pl.when(has_next)
    def _():
        deliver(1, mid_b, table_b, pick_b, grad_out, 1, 1 + quarter)

    @pl.when(has_next)
    def _():
        deliver(1, mid_b, table_b, pick_b, grad_out, 1 + quarter, 1 + 2 * quarter)

    chains(2)

    @pl.when(has_next)
    def _():
        deliver(1, mid_b, table_b, pick_b, grad_out, 1 + 2 * quarter, 1 + 3 * quarter)

    chains(3)

    @pl.when(has_next)
    def _():
        deliver(1, mid_b, table_b, pick_b, grad_out, 1 + 3 * quarter, spread)

    @pl.when(s == sections - 1)
    def _():
        clear(1, pick_b, grad_out)


    arrived(chain_a.at[far_a - 1], a_recv.at[far_a - 1])
    total = piece[c, x, y] + chain_a[far_a - 1].astype(f32)
    if far_b:
        arrived(chain_b.at[far_b - 1], b_recv.at[far_b - 1])
        total = total + chain_b[far_b - 1].astype(f32)
    total = total * (1.0 / peers)
    final[...] = total
    final_gain[...] = jnp.sum(total[2 * share :, :share], axis=0, keepdims=True)
    stores = (
        pltpu.make_async_copy(final.at[pl.ds(0, share)], gdown_out, load_sem.at[0]),
        pltpu.make_async_copy(final.at[pl.ds(share, share)], gup_out, load_sem.at[1]),
        pltpu.make_async_copy(final_gain, ggain_out, load_sem.at[2]),
    )
    for store in stores:
        store.start()

    for k, half in enumerate((1 - x, x)):
        arrived(from_core.at[half], core_send.at[k])
    arrived(from_x, x_send)
    for t in range(far_a):
        arrived(chain_a.at[t], a_send.at[t])
    for t in range(far_b):
        arrived(chain_b.at[t], b_send.at[t])
    arrived(tiles_hop.at[pl.ds(0, spread - 1)], tile_send)

    for store in stores:
        store.wait()

    def settle_out(way, src):
        arrived(src.at[pl.ds(0, spread - 1)], p1_send.at[way])
        arrived(src, z_send.at[way])
        arrived(tiles_hop, tz_send.at[way])

    def settle_in(way, mid, tiles, pick, out):
        keep(way, pick, out, m).wait()
        arrived(half_of(mid, c), swap_send.at[way])
        arrived(tiles.at[c], tswap_send.at[way])
        arrived(pick.at[pl.ds(0, spread - 1)], p2_send.at[way])
        arrived(pick.at[pl.ds(0, spread - 1)], p2_recv.at[way])

    @pl.when(has_next)
    def _():
        settle_out(0, src_f)

    @pl.when(has_prev)
    def _():
        settle_out(1, src_b)

    @pl.when(has_prev)
    def _():
        settle_in(0, mid_f, tiles_f, pick_f, act_out)

    @pl.when(has_next)
    def _():
        settle_in(1, mid_b, tiles_b, pick_b, grad_out)


def place(*refs):
    count = (len(refs) - 2) // 3
    given, results, held = (refs[k * count : (k + 1) * count] for k in range(3))
    load_sem, store_sem = refs[-2:]
    slots = given[0].shape[0]
    parts = [(k, pl.ds(i, 1)) for i in range(slots) for k in (0, 1)]
    parts += [(k, slice(None)) for k in range(2, count)]
    loads, stores = [], []
    for n, (k, cut) in enumerate(parts):
        loads.append(pltpu.make_async_copy(given[k].at[cut], held[k].at[cut], load_sem.at[n]))
        stores.append(pltpu.make_async_copy(held[k].at[cut], results[k].at[cut], store_sem.at[n]))
    for load in loads:
        load.start()
    for load, store in zip(loads, stores):
        load.wait()
        store.start()
    for store in stores:
        store.wait()


def on_device(sections, peers, acts, cotangent, gain, w_down, w_up, route_fwd, route_bwd, token_counts):
    batches, length, width = acts.shape[2:]
    units = w_up.shape[1]
    cap = batches + batches // 2
    rows = batches * length
    spread = peers // 2
    ring = spread // 2
    group = 16
    span = width // (spread // (length // group))
    share = width // peers
    height = 2 * share + group
    far_a, far_b = ring // 2, max(ring - 1 - ring // 2, 1)
    vmem, smem = pltpu.VMEM, pltpu.SMEM
    dma, pair = pltpu.SemaphoreType.DMA, pltpu.SemaphoreType.DMA((2,))
    in_hbm = pl.BlockSpec(memory_space=pltpu.HBM)
    mid = vmem((1 + 2 * spread * batches, group, span), bf16)
    pick = vmem((spread, cap, group, span), bf16)
    src = vmem((spread, batches, group, span), bf16)
    shapes = (
        jax.ShapeDtypeStruct((cap, length, width), bf16),
        jax.ShapeDtypeStruct((cap, length, width), bf16),
        jax.ShapeDtypeStruct((share, units), f32),
        jax.ShapeDtypeStruct((share, units), f32),
        jax.ShapeDtypeStruct((1, share), f32),
    )
    results = pl.pallas_call(
        functools.partial(kernel, sections, peers, cap),
        out_shape=shapes,
        in_specs=[in_hbm] * 8,
        out_specs=(in_hbm,) * 5,
        scratch_shapes=[
            smem((batches,), i32), smem((batches,), i32), smem((batches,), i32),
            vmem((rows, width), bf16), vmem((rows, width), bf16), vmem((1, width), f32),
            vmem((width, units), bf16), vmem((units, width), bf16),
            vmem((rows, width), bf16),
            vmem((rows, width), bf16),
            vmem((rows, width), f32),
            vmem((rows, 1), f32),
            vmem((group, width), f32),
            src, src, src, src, mid, mid, pick, pick,
            vmem((8, 128), i32), vmem((spread, 8, 128), i32),
            vmem((2, spread, 8, 128), i32), vmem((2, spread, 8, 128), i32),
            vmem((8, 128), i32), smem((8, 128), i32), smem((8, 128), i32),
            vmem((2, 2, ring, height, units), f32),
            vmem((2, ring, height, units), f32),
            vmem((ring, height, units), bf16), vmem((ring, height, units), bf16),
            vmem((far_a, height, units), bf16), vmem((far_b, height, units), bf16),
            vmem((far_a, height, units), bf16), vmem((far_b, height, units), bf16),
            vmem((height, units), f32), vmem((1, share), f32),
            pltpu.SemaphoreType.REGULAR, dma((2, spread)), dma((8,)), pair, dma((2, spread)), pair, dma((2, spread)), pair, pair,
            dma, dma, pair, pair, pair, pair,
            pair, pair, pair,
            pair, pair, dma, dma, dma((far_a,)), dma((far_a,)), dma((far_b,)), dma((far_b,)),
        ],
        compiler_params=pltpu.CompilerParams(
            collective_id=0, has_side_effects=True, vmem_limit_bytes=60 * 1024 * 1024
        ),
        cost_estimate=pl.CostEstimate(
            flops=12 * rows * width * units, bytes_accessed=8 * rows * width, transcendentals=rows * units
        ),
        name="adapter_relay",
    )(
        route_fwd.reshape(batches), route_bwd.reshape(batches), token_counts.reshape(batches),
        acts.reshape(rows, width), cotangent.reshape(rows, width), gain, w_down[0], w_up[0],
    )
    arrived_act, arrived_grad, grad_down, grad_up, grad_gain = pl.pallas_call(
        place,
        out_shape=shapes,
        in_specs=[in_hbm] * 5,
        out_specs=(in_hbm,) * 5,
        scratch_shapes=[vmem(made.shape, made.dtype) for made in shapes] + [dma((2 * cap + 3,)), dma((2 * cap + 3,))],
        compiler_params=pltpu.CompilerParams(vmem_limit_bytes=60 * 1024 * 1024),
        name="place_results",
    )(*results)
    return arrived_act[None, None], arrived_grad[None, None], grad_down[None], grad_up.T[None], grad_gain


def solution(mesh):
    placed = (
        P("section", "peer", None, None, None),
        P("section", "peer", None, None, None),
        P("section", None),
        P("section", None, None),
        P("section", None, None),
        P("section", "peer", None),
        P("section", "peer", None),
        P("section", "peer", None),
    )
    return jax.shard_map(
        functools.partial(on_device, mesh.shape["section"], mesh.shape["peer"]),
        mesh=mesh,
        in_specs=placed,
        out_specs=(
            P("section", "peer", None, None, None),
            P("section", "peer", None, None, None),
            P("section", "peer", None),
            P("section", None, "peer"),
            P("section", "peer"),
        ),
        check_vma=False,
    )
```
